512 devices in a mesh: grp: 16 (over x, y), row: 8 (over z_hi, core), col: 4 (over z_lo).
Axes of the slice: x: 4, y: 4, z: 16 (z_hi: 4, z_lo: 4; z = z_hi * 4 + z_lo), core: 2. Of those that a mesh axis runs over, the one named last changes fastest.
Arguments:
- coherency: bfloat16 [32, 8, 16, 512, 512], P('grp', None, None, 'row', 'col'), may hold values from -0.125 to 0.125
- station_gains: float32 [32, 8, 16, 512], P('grp', None, None, ('row', 'col')), may hold values from -6 to 6
- tangent: float32 [32, 8, 16, 512], P('grp', None, None, ('row', 'col')), may hold values from -6 to 6
- flag_mask: int32 [512, 512], P('row', 'col'), may hold values 0 or 1
- station_order: int32 [512], replicated, may hold values from 0 to 511, each once
Outputs:
- hessian_product: float32 [32, 8, 16, 512], P('grp', None, None, ('row', 'col'))
The draws below stay inside these ranges and needn't reach their ends.
Inputs may be any that keep to these rules, and one draw needn't show every extreme that they name: `station_order`: each station stands at exactly one position.
All inputs are finite; a program needn't handle non-finite values. No bound on the sum of `flag_mask` on one device may be relied on, other than what follows from the above.
Results may differ from the reference program's by a relative error of at most 0.0003.
Values sent between devices are 32-bit elements; how exact they have to be, the bound alone decides.
A program may use at most 64 MiB of HBM per device.

```python
import jax
import jax.numpy as jnp
from jax import lax

S = 512
D = 16
POLY = 4
F = 32


def place_ends(result, own_key, smallest, largest):
    longest = result.shape.index(max(result.shape))
    spots = []
    for shift in (0, 1):
        where = [jax.random.randint(jax.random.fold_in(own_key, axis), (), 0, length) for axis, length in enumerate(result.shape)]
        where[longest] = (where[longest] + shift) % result.shape[longest]
        spots.append(tuple(where))
    return result.at[spots[0]].set(smallest).at[spots[1]].set(largest)


def levels(own_key, shape, cuts, low, high):
    def one(dim, parts):
        heights = jax.random.uniform(jax.random.fold_in(jax.random.fold_in(own_key, 6), dim), (parts,), jnp.float32, low / len(cuts), high / len(cuts))
        return jnp.repeat(jnp.exp(heights), shape[dim] // parts).reshape((-1,) + (1,) * (len(shape) - dim - 1))

    level = one(*cuts[0])
    for cut in cuts[1:]:
        level = level * one(*cut)
    return level


def scatter_about(stream_key, extent, deviation, reach, split=(), dtype=jnp.bfloat16):
    entries = jax.random.normal(stream_key, extent, jnp.float32) * deviation
    if len(split) > 0:
        entries = levels(stream_key, extent, split, -0.22, 0.18) * entries
    return jnp.clip(entries, min=-reach, max=reach).astype(dtype)


def setup_inputs(seed: int = 0) -> dict:
    seeds = jax.random.split(jax.random.key(seed), 6)
    return {
        "coherency": scatter_about(seeds[0], (F, 8, D, S, S), 0.02, 0.125, ((0, 16), (3, 8), (4, 4))),
        "station_gains": scatter_about(seeds[1], (F, 8, D, S), 1.0, 6.0, ((0, 16), (3, 32)), jnp.float32),
        "tangent": scatter_about(seeds[2], (F, 8, D, S), 1.0, 6.0, ((0, 16), (3, 32)), jnp.float32),
        "flag_mask": place_ends((jax.random.randint(seeds[3], (S, S), 0, 8) < 7).astype(jnp.int32), jax.random.fold_in(seeds[3], 1), 0, 1),
        "station_order": jax.random.permutation(seeds[4], S).astype(jnp.int32),
    }


consensus_weight = 1.0

def as_blocks(packed):
    return packed.reshape((2, 2, 2) + packed.shape[1:])

def from_blocks(blocks):
    return blocks.reshape((8,) + blocks.shape[3:])

def conj_transpose(blocks):
    return jnp.stack([jnp.swapaxes(blocks[0], 0, 1), -jnp.swapaxes(blocks[1], 0, 1)])

def complex_product(left_side, right_side):
    real_rows = []
    imag_rows = []
    for left_row in range(2):
        real_row = []
        imag_row = []
        for right_col in range(2):
            real_sum = 0.0
            imag_sum = 0.0
            for middle in range(2):
                left_real = left_side[0, left_row, middle]
                left_imag = left_side[1, left_row, middle]
                right_real = right_side[0, middle, right_col]
                right_imag = right_side[1, middle, right_col]
                real_sum = real_sum + left_real * right_real - left_imag * right_imag
                imag_sum = imag_sum + left_real * right_imag + left_imag * right_real
            real_row.append(real_sum)
            imag_row.append(imag_sum)
        real_rows.append(jnp.stack(real_row))
        imag_rows.append(jnp.stack(imag_row))
    return jnp.stack([jnp.stack(real_rows), jnp.stack(imag_rows)])

def make_basis(count):
    frequency = -1.0 + (2.0 * jnp.arange(count).astype(jnp.float32) + 1.0) / count
    columns = [jnp.ones_like(frequency)]
    for degree in range(1, POLY):
        columns.append(columns[-1] * frequency)
    return jnp.stack(columns, axis=1)

def solve_coefficients(freq_basis, moments):
    gram_matrix = jnp.dot(freq_basis.T, freq_basis, precision=lax.Precision.HIGHEST)
    factor = jnp.linalg.cholesky(gram_matrix)
    flattened = moments.reshape(moments.shape[0], -1)
    solved = jax.scipy.linalg.cho_solve((factor, True), flattened)
    return solved.reshape(moments.shape)

def direction_models(slices):
    coh_dir, gain_dir, tan_dir = slices
    coherent = as_blocks(coh_dir.astype(jnp.float32))
    gain_blocks = as_blocks(gain_dir)
    tan_blocks = as_blocks(tan_dir)
    model_left = complex_product(gain_blocks[..., :, None], coherent)
    model_right = complex_product(coherent, conj_transpose(gain_blocks[..., None, :]))
    return (model_left, model_right, tan_blocks)

def channel_term(block, gain_tile, tangent_tile, weight):
    slices = (jnp.moveaxis(block, 1, 0), jnp.moveaxis(gain_tile, 1, 0), jnp.moveaxis(tangent_tile, 1, 0))

    def forward(accumulated, slice_in):
        model_left, model_right, tan_blocks = direction_models(slice_in)
        change = complex_product(tan_blocks[..., :, None], model_right)
        change = change + complex_product(model_left, conj_transpose(tan_blocks[..., None, :]))
        return (accumulated + change, None)
    accumulated, _ = lax.scan(forward, jnp.zeros((2, 2, 2, S, S), jnp.float32), slices)
    weighted = accumulated * weight

    def backward(slice_in):
        model_left, model_right, tan_blocks = direction_models(slice_in)
        row_part = jnp.sum(complex_product(weighted, conj_transpose(model_right)), axis=-1)
        col_part = jnp.sum(complex_product(conj_transpose(weighted), model_left), axis=-2)
        return from_blocks(row_part + col_part)
    grads = lax.map(backward, slices)
    return jnp.moveaxis(grads, 0, 1)

def reference(coherency, station_gains, tangent, flag_mask, station_order):
    gain_tile = jnp.take(station_gains, station_order, axis=3)
    tangent_tile = jnp.take(tangent, station_order, axis=3)
    weight = flag_mask.astype(jnp.float32)
    tile_grad = lax.map(lambda slices: channel_term(slices[0], slices[1], slices[2], weight), (coherency, gain_tile, tangent_tile))
    data_term = jnp.zeros_like(tangent).at[:, :, :, station_order].set(tile_grad)
    freq_basis = make_basis(F)
    moments = jnp.einsum('fk,fcds->kcds', freq_basis, tangent, precision=lax.Precision.HIGHEST)
    coefficients = solve_coefficients(freq_basis, moments)
    smooth = jnp.einsum('fk,kcds->fcds', freq_basis, coefficients, precision=lax.Precision.HIGHEST)
    return data_term + consensus_weight * (tangent - smooth)
```

```python
import functools

import jax
import jax.numpy as jnp
import numpy as np
from jax import lax
from jax.experimental import pallas as pl
from jax.experimental.pallas import tpu as pltpu
from jax.sharding import PartitionSpec as P

POLY = 4
CONSENSUS_WEIGHT = 1.0
MESH = pl.DeviceIdType.MESH

COMPS = 8
CHIPS = 16
HALF = CHIPS // 2
NEAR = 4


def smooth_basis(count):
    frequency = -1.0 + (2.0 * np.arange(count) + 1.0) / count
    factor = np.linalg.cholesky(np.linalg.inv(np.vander(frequency, POLY, True).T @ np.vander(frequency, POLY, True))[::-1, ::-1])
    return [[float(value) for value in row] for row in factor.T[::-1, ::-1]]


class Place:
    def __init__(self):
        row, col = lax.axis_index("row"), lax.axis_index("col")
        self.core = lax.rem(row, 2)
        self.chip = (row // 2) * NEAR + col

    def at(self, step):
        return lax.rem(self.chip + (step + CHIPS), CHIPS)

    def neighbour(self, step):
        chip = self.at(step)
        return {"row": (chip // NEAR) * 2 + self.core, "col": lax.rem(chip, NEAR)}

    def sibling(self):
        chip = self.chip
        return {"row": (chip // NEAR) * 2 + (1 - self.core), "col": lax.rem(chip, NEAR)}


def entry(matrix, row, col, turned):
    if turned:
        return matrix[2 * col + row], matrix[4 + 2 * col + row], -1
    return matrix[2 * row + col], matrix[4 + 2 * row + col], 1


def add(total, term, sign):
    if total is None:
        return term if sign > 0 else -term
    return total + term if sign > 0 else total - term


def product(left_side, right_side, start=None, left_turned=False, right_turned=False):
    result = [None] * 8
    for row in range(2):
        for col in range(2):
            real, imag = (None, None) if start is None else (start[2 * row + col], start[4 + 2 * row + col])
            for middle in range(2):
                lr, li, ls = entry(left_side, row, middle, left_turned)
                rr, ri, rs = entry(right_side, middle, col, right_turned)
                real = add(add(real, lr * rr, 1), li * ri, -ls * rs)
                terms = [(lr * ri, rs), (li * rr, ls)]
                for term, sign in sorted(terms, key=lambda pair: -pair[1]):
                    imag = add(imag, term, sign)
            result[2 * row + col] = real
            result[4 + 2 * row + col] = imag
    return result


def split(value):
    high = value.astype(jnp.bfloat16)
    return high, (value - high.astype(jnp.float32)).astype(jnp.bfloat16)


def dot(left_side, right_side):
    return jnp.dot(left_side, right_side, preferred_element_type=jnp.float32)


ROWS = 16


REACH = 3
FAR = 4


def kernel(groups, gain_in, tan_in, order_in, flag_in, coh_in, out_ref,
           gain_ref, tan_ref, order_ref, flag_ref, coh_ref, all_ref, peer_buf, resid_ref,
           pick_ref, place_ref, mix_ref, gj_ref, left_ref, right_ref, row_ref, col_ref,
           part_ref, from_sib, total, far_buf, near_buf,
           in_sem, coh_sem, send_z, recv_z, send_s, recv_s, send_g, recv_g, send_w, recv_w, send_f, recv_f, send_n, recv_n):
    channels, comps, directions, tile_rows, tile_cols = coh_ref.shape
    stations = pick_ref.shape[1]
    values = comps * directions
    owned = gain_ref.shape[2]
    strips = tile_rows // ROWS
    place = Place()
    grp, row, col = lax.axis_index("grp"), lax.axis_index("row"), lax.axis_index("col")
    sibling = place.sibling()

    inputs = [
        pltpu.make_async_copy(source, target, in_sem.at[n])
        for n, (source, target) in enumerate(((gain_in, gain_ref), (tan_in, tan_ref), (order_in, order_ref), (flag_in, flag_ref)))
    ]
    for copy in inputs:
        copy.start()

    def peer(step):
        return {"grp": lax.rem(grp + (step + groups), groups)}

    partners = [place.neighbour(way * step) for step in range(1, max(REACH, FAR) + 1) for way in (1, -1)]
    partners = partners + [sibling] + [peer(step) for step in range(1, groups)]
    barrier = pltpu.get_barrier_semaphore()
    for device in partners:
        pl.semaphore_signal(barrier, inc=1, device_id=device, device_id_type=MESH)


    def block(channel, chip, core):
        start = pl.multiple_of(lax.rem(chip, NEAR) * owned, owned)
        return all_ref.at[channel, chip // NEAR, core, pl.ds(start, owned), :]

    def block_copy(channel, origin, core, target, send_sem, recv_sem):
        chip = place.at(origin)
        return pltpu.make_async_remote_copy(
            src_ref=block(channel, chip, core), dst_ref=block(channel, chip, core),
            send_sem=send_sem, recv_sem=recv_sem, device_id=target, device_id_type=MESH,
        )

    def limit(way):
        return HALF if way > 0 else HALF - 1

    def pass_on(channel, way, done):
        copies = []
        for step in range(REACH, 0, -1):
            if done + step <= limit(way):
                slot = HALF + way * (done + step)
                copies.append(block_copy(
                    channel, -way * done, place.core, place.neighbour(way * step), send_z.at[channel, slot], recv_z.at[channel, slot]
                ))
        return copies

    def to_sibling(channel, offset):
        slot = HALF + offset
        return block_copy(channel, -offset, place.core, sibling, send_s.at[channel, slot], recv_s.at[channel, slot])

    def from_ring(channel, offset):
        slot = HALF + offset
        return block_copy(channel, -offset, place.core, sibling, send_z.at[channel, slot], recv_z.at[channel, slot])

    def from_sibling(channel, offset):
        slot = HALF + offset
        return block_copy(channel, -offset, 1 - place.core, sibling, send_s.at[channel, slot], recv_s.at[channel, slot])

    offsets = range(1 - HALF, HALF + 1)
    stages = -(-HALF // REACH)

    def begin_gather(channel):
        for copy in pass_on(channel, 1, 0) + pass_on(channel, -1, 0) + [to_sibling(channel, 0)]:
            copy.start()

    def gather_stage(channel, stage):
        for distance in range(min((stage + 1) * REACH, HALF), stage * REACH, -1):
            for way in (1, -1):
                if distance <= limit(way):
                    from_ring(channel, way * distance).wait_recv()
                    if distance % REACH == 0:
                        for copy in pass_on(channel, way, distance):
                            copy.start()
                    to_sibling(channel, way * distance).start()

    def end_gather(channel):
        for offset in offsets:
            from_sibling(channel, offset).wait_recv()

    def to_peer(step):
        return pltpu.make_async_remote_copy(
            src_ref=peer_buf.at[0], dst_ref=peer_buf.at[step],
            send_sem=send_g.at[step], recv_sem=recv_g.at[step], device_id=peer(step), device_id_type=MESH,
        )

    def gather_sends(channel):
        copies = [to_sibling(channel, offset) for offset in offsets]
        for way in (1, -1):
            for done in range(0, limit(way), REACH):
                copies += pass_on(channel, way, done)
        return copies


    def rows_of(step):
        chip = place.at(step)
        return chip // NEAR, pl.ds(pl.multiple_of(lax.rem(chip, NEAR) * owned, owned), owned)

    def sums_for(channel, step):
        run, rows = rows_of(step)
        return total.at[channel, run, rows, :]

    def swap(channel):
        return pltpu.make_async_remote_copy(
            src_ref=part_ref.at[channel, :, 1 - place.core], dst_ref=from_sib.at[channel],
            send_sem=send_w.at[channel], recv_sem=recv_w.at[channel], device_id=sibling, device_id_type=MESH,
        )

    def hop(channel, source, buffer, slot, sends, recvs, step):
        return pltpu.make_async_remote_copy(
            src_ref=source, dst_ref=buffer.at[channel, slot], send_sem=sends.at[channel, slot], recv_sem=recvs.at[channel, slot],
            device_id=place.neighbour(step), device_id_type=MESH,
        )

    reaches = ((1, HALF - FAR), (-1, HALF - 1 - FAR))

    def to_add(channel):
        return {
            way * step: hop(channel, sums_for(channel, way * (step + FAR)), far_buf, FAR + way * step, send_f, recv_f, way * step)
            for way, most in reaches for step in range(most, 0, -1)
        }

    def direct(channel):
        return {
            way * step: hop(channel, sums_for(channel, way * step), near_buf, FAR + way * step, send_n, recv_n, way * step)
            for step in range(1, FAR) for way in (1, -1)
        }

    def added(channel):
        return {
            way * FAR: hop(channel, far_buf.at[channel, FAR if way > 0 else 2 * FAR + 1], near_buf, FAR + way * FAR, send_n, recv_n, way * FAR)
            for way in (1, -1)
        }

    def send_sums(channel):
        swap(channel).wait_recv()
        total[channel] = part_ref[channel, :, place.core] + from_sib[channel]
        for copy in list(to_add(channel).values()) + list(direct(channel).values()):
            copy.start()

    def send_added(channel):
        arrivals = to_add(channel)
        for (way, most), copy in zip(reaches, added(channel).values()):
            run, rows = rows_of(way * FAR)
            gathered = total[channel, run, rows, :]
            for step in range(1, most + 1):
                arrivals[way * step].wait_recv()
                gathered = gathered + far_buf[channel, FAR + way * step]
            far_buf[channel, FAR if way > 0 else 2 * FAR + 1] = gathered
            copy.start()

    def finish(channel):
        run, rows = rows_of(0)
        summed = total[channel, run, rows, :] + resid_ref[channel]
        for copy in list(direct(channel).values()) + list(added(channel).values()):
            copy.wait_recv()
        for slot in range(2 * FAR + 1):
            if slot != FAR:
                summed = summed + near_buf[channel, slot]
        out_ref[channel] = summed.T

    def sum_sends(channel):
        return [swap(channel)] + list(to_add(channel).values()) + list(direct(channel).values()) + list(added(channel).values())


    basis = smooth_basis(channels * groups)

    def heights(group, channel):
        frequency = (group * channels + channel).astype(jnp.float32) * (2.0 / (channels * groups)) + (1.0 / (channels * groups) - 1.0)
        powers = [1.0]
        for _ in range(1, POLY):
            powers.append(powers[-1] * frequency)
        return [sum(line[k] * powers[k] for k in range(POLY) if abs(line[k]) > 1e-9) for line in basis]

    def consensus():
        moments = [jnp.zeros((owned, values), jnp.float32) for _ in range(POLY)]
        for step in range(groups):
            if step > 0:
                to_peer(step).wait_recv()
            origin = lax.rem(grp + (groups - step), groups)
            for source in range(channels):
                seen = peer_buf[step, source]
                for k, height in enumerate(heights(origin, source)):
                    moments[k] = moments[k] + height * seen
        for channel in range(channels):
            smooth = sum(height * moment for height, moment in zip(heights(grp, channel), moments))
            resid_ref[channel] = CONSENSUS_WEIGHT * (peer_buf[0, channel] - smooth)


    lane = lax.broadcasted_iota(jnp.int32, (ROWS, 128), 1)
    same_row = (lane & (ROWS - 1)) == lax.broadcasted_iota(jnp.int32, (ROWS, 128), 0)

    def as_mask(hit):
        return hit.astype(jnp.float32).astype(jnp.bfloat16)

    def one_hots():
        col_ids = order_ref[pl.ds(col, 1), :]
        row_ids = order_ref[pl.ds(row // 2, 1), :]
        row_ids = jnp.where(lax.rem(row, 2) == 1, pltpu.roll(row_ids, tile_rows, 1), row_ids)
        for n, ids in enumerate((col_ids, row_ids)):
            ids = jnp.broadcast_to(ids, (128, 128))
            turned = ids.astype(jnp.float32).T.astype(jnp.int32)
            count = (tile_cols, tile_rows)[n]
            for tile in range(stations // 128):
                spot = lax.broadcasted_iota(jnp.int32, (128, 128), 1) + tile * 128
                pick_ref[n * tile_cols:n * tile_cols + count, tile * 128:(tile + 1) * 128] = as_mask(turned == spot)[:count]
                spot = lax.broadcasted_iota(jnp.int32, (128, 128), 0) + tile * 128
                place_ref[tile * 128:(tile + 1) * 128, n * 128:(n + 1) * 128] = as_mask(ids == spot)

    def prologue(channel):
        parts = split(all_ref[channel].reshape(stations, 2 * values))
        chosen = [dot(pick_ref[...], part) for part in parts]

        chosen_cols = chosen[0][:tile_cols] + chosen[1][:tile_cols]
        for array in range(2):
            turned = chosen_cols[:, array * values:(array + 1) * values].T
            gj_ref[pl.ds(array * comps, comps)] = turned.reshape(comps, directions, tile_cols)

        sides = [[
            one[tile_cols:, array * values:(array + 1) * values].T.reshape(comps, directions, tile_rows) for array in range(2)
        ] for one in chosen]
        for index in range(strips):
            lanes = slice(index * ROWS, (index + 1) * ROWS)
            for array in range(2):
                for line in range(2):
                    for part in range(2):
                        pieces = []
                        for side in sides:
                            for middle in range(2):
                                for other in range(2):
                                    value = side[array][4 * (part ^ other) + 2 * line + middle][:, lanes]
                                    pieces.append(-value if (part, other) == (0, 1) else value)
                        mix_ref[index, 4 * array + 2 * line + part] = jnp.concatenate(pieces, axis=1)
        col_ref[...] = jnp.zeros_like(col_ref)

    def strip(channel, index):
        rows = pl.ds(pl.multiple_of(index * ROWS, ROWS), ROWS)

        def forward(direction, change):
            here = pl.ds(direction, 1)
            coherent = [coh_ref[channel, comp, direction, rows, :] for comp in range(comps)]
            stacked = jnp.concatenate([
                jnp.concatenate([coherent[4 * part + 2 * middle], coherent[4 * part + 2 * middle + 1]], axis=1)
                for middle in range(2) for part in range(2)
            ], axis=0)
            mixing = jnp.concatenate([
                jnp.where(same_row, mix_ref[index, n, here, :], 0.0).astype(jnp.bfloat16) for n in range(8)
            ], axis=0)
            models = dot(mixing, jnp.concatenate([stacked, stacked], axis=0))

            def model(array):
                return [
                    models[ROWS * (4 * array + 2 * line + part):ROWS * (4 * array + 2 * line + part + 1), end * 128:(end + 1) * 128]
                    for part in range(2) for line in range(2) for end in range(2)
                ]

            model_left, tan_left = model(0), model(1)
            gain_j = [gj_ref[comp, here, :] for comp in range(comps)]
            tan_j = [gj_ref[comps + comp, here, :] for comp in range(comps)]
            for comp in range(comps):
                left_ref[comp, direction] = model_left[comp]
            change = product(tan_left, gain_j, change, right_turned=True)
            change = product(model_left, tan_j, change, right_turned=True)
            model_right = product([value.astype(jnp.float32) for value in coherent], gain_j, right_turned=True)
            for part in range(2):
                for line in range(2):
                    for end in range(2):
                        for n, piece in enumerate(split(model_right[4 * part + 2 * line + end])):
                            right_ref[4 * n + 2 * line + part, direction, :, end * 128:(end + 1) * 128] = piece
            return tuple(change)

        zero = jnp.zeros((ROWS, tile_cols), jnp.float32)
        change = lax.fori_loop(0, directions, forward, (zero,) * comps, unroll=4)
        weight = flag_ref[rows, :].astype(jnp.float32)
        weighted = [value * weight for value in change]

        pieces = [split(value) for value in weighted]
        lines = jnp.concatenate([
            jnp.concatenate([pieces[4 * part + 2 * line][n], pieces[4 * part + 2 * line + 1][n]], axis=1)
            for n in range(2) for line in range(2) for part in range(2)
        ], axis=0)
        pairs = lax.dot_general(
            right_ref[...].reshape(2 * 4 * directions * ROWS, 2 * tile_cols), lines, (((1,), (1,)), ((), ())), preferred_element_type=jnp.float32
        ).reshape(2, 4, directions, ROWS, 128)
        for n in range(4):
            kept = jnp.where(same_row[None], pairs[0, n] + pairs[1, n], 0.0)
            row_ref[index, n] = jnp.sum(kept, axis=1)

        def backward(direction, _):
            model_left = [left_ref[comp, direction] for comp in range(comps)]
            terms = product(weighted, model_left, left_turned=True)
            for comp in range(comps):
                folded = terms[comp][:8]
                for part in range(1, ROWS // 8):
                    folded = folded + terms[comp][8 * part:8 * part + 8]
                col_ref[comp, direction] += folded
            return 0

        lax.fori_loop(0, directions, backward, 0, unroll=4)

    def epilogue(channel):
        sums = [[row_ref[index, n] for n in range(4)] for index in range(strips)]
        sums = [[value[:, :64] + value[:, 64:] for value in line] for line in sums]

        def cut(value, line, part):
            return value[:, (2 * line + part) * ROWS:(2 * line + part + 1) * ROWS]

        by_comp = []
        for part in range(2):
            for line in range(2):
                for end in range(2):
                    pieces = []
                    for value in sums:
                        if part == 0:
                            pieces.append(cut(value[2 * end], line, 0) + cut(value[2 * end + 1], line, 1))
                        else:
                            pieces.append(cut(value[2 * end], line, 1) - cut(value[2 * end + 1], line, 0))
                    by_comp.append(jnp.concatenate(pieces, axis=1))
        row_sums = jnp.concatenate(by_comp, axis=0)
        col_sums = jnp.sum(col_ref[...], axis=2).reshape(values, tile_cols)
        placed = jnp.zeros((stations, values), jnp.float32)
        for part in split(jnp.concatenate([col_sums, row_sums], axis=1)):
            placed = placed + lax.dot_general(
                place_ref[:, :tile_cols + tile_rows], part, (((1,), (1,)), ((), ())), preferred_element_type=jnp.float32
            )
        part_ref[channel] = placed.reshape(part_ref.shape[1:])
        swap(channel).start()


    inputs[0].wait()
    inputs[1].wait()
    own_start = pl.multiple_of(lax.rem(place.chip, NEAR) * owned, owned)
    for channel in range(channels):
        tan_t = tan_ref[channel].T
        peer_buf[0, channel] = tan_t
        own = all_ref.at[channel, place.chip // NEAR, place.core, pl.ds(own_start, owned), :]
        own[:, :values] = gain_ref[channel].T
        own[:, values:] = tan_t
    pl.semaphore_wait(barrier, len(partners))
    begin_gather(0)
    coherency = [pltpu.make_async_copy(coh_in.at[channel], coh_ref.at[channel], coh_sem.at[channel]) for channel in range(channels)]
    for copy in coherency:
        copy.start()
    inputs[2].wait()
    inputs[3].wait()
    one_hots()
    gather_stage(0, 0)
    begin_gather(1)
    for step in range(1, groups):
        to_peer(step).start()
    for stage in range(1, stages):
        gather_stage(0, stage)
    end_gather(0)
    for copy in coherency:
        copy.wait()

    def work(channel, _):
        @pl.when(channel == 1)
        def _():
            end_gather(1)

        prologue(channel)

        def one(index, _):
            for stage in range(stages):
                @pl.when(jnp.logical_and(channel == 0, index == stage))
                def _():
                    gather_stage(1, stage)

            @pl.when(jnp.logical_and(channel == 1, index == 0))
            def _():
                send_sums(0)

            @pl.when(jnp.logical_and(channel == 1, index == 1))
            def _():
                consensus()

            @pl.when(jnp.logical_and(channel == 1, index == 3))
            def _():
                send_added(0)

            strip(channel, index)
            return 0

        lax.fori_loop(0, strips, one, 0)
        epilogue(channel)
        return 0

    lax.fori_loop(0, channels, work, 0)
    send_sums(1)
    finish(0)
    send_added(1)
    finish(1)
    for channel in range(channels):
        for copy in gather_sends(channel) + sum_sends(channel):
            copy.wait_send()
    for step in range(1, groups):
        to_peer(step).wait_send()


def on_device(groups, coherency, station_gains, tangent, flag_mask, station_order):
    channels, comps, directions, tile_rows, tile_cols = coherency.shape
    owned = tangent.shape[3]
    stations = station_order.shape[0]
    values = comps * directions
    runs = CHIPS // NEAR
    near = NEAR * owned
    strips = tile_rows // ROWS
    vmem = pltpu.VMEM
    f32, bf16 = jnp.float32, jnp.bfloat16

    def sems(*shape):
        return pltpu.SemaphoreType.DMA(shape)

    hbm = pl.BlockSpec(memory_space=pl.ANY)
    result = pl.pallas_call(
        functools.partial(kernel, groups),
        out_shape=jax.ShapeDtypeStruct((channels, values, owned), f32),
        in_specs=[hbm] * 5,
        out_specs=pl.BlockSpec(memory_space=pltpu.VMEM),
        scratch_shapes=[
            vmem((channels, values, owned), f32),
            vmem((channels, values, owned), f32),
            vmem((stations // 128, 128), jnp.int32),
            vmem((tile_rows, tile_cols), jnp.int32),
            vmem(coherency.shape, bf16),
            vmem((channels, runs, 2, near, 2 * values), f32),
            vmem((groups, channels, owned, values), f32),
            vmem((channels, owned, values), f32),
            vmem((tile_cols + tile_rows, stations), bf16),
            vmem((stations, 256), bf16),
            vmem((strips, comps, directions, 128), f32),
            vmem((2 * comps, directions, tile_cols), f32),
            vmem((comps, directions, ROWS, tile_cols), f32),
            vmem((comps, directions, ROWS, 2 * tile_cols), bf16),
            vmem((strips, 4, directions, 128), f32),
            vmem((comps, directions, 8, tile_cols), f32),
            vmem((channels, runs, 2, near, values), f32),
            vmem((channels, runs, near, values), f32),
            vmem((channels, runs, near, values), f32),
            vmem((channels, 2 * FAR + 2, owned, values), f32),
            vmem((channels, 2 * FAR + 1, owned, values), f32),
            sems(4), sems(channels),
            sems(channels, CHIPS + 1), sems(channels, CHIPS + 1), sems(channels, CHIPS + 1), sems(channels, CHIPS + 1),
            sems(groups), sems(groups), sems(channels), sems(channels),
            sems(channels, 2 * FAR + 1), sems(channels, 2 * FAR + 1), sems(channels, 2 * FAR + 1), sems(channels, 2 * FAR + 1),
        ],
        compiler_params=pltpu.CompilerParams(collective_id=0, has_side_effects=True, vmem_limit_bytes=56 << 20),
        name="hessian",
    )(
        station_gains.reshape(channels, values, owned),
        tangent.reshape(channels, values, owned),
        station_order.reshape(stations // 128, 128),
        flag_mask,
        coherency,
    )
    return result.reshape(channels, comps, directions, owned)


def solution(mesh):
    in_specs = (
        P("grp", None, None, "row", "col"),
        P("grp", None, None, ("row", "col")),
        P("grp", None, None, ("row", "col")),
        P("row", "col"),
        P(),
    )
    out_specs = P("grp", None, None, ("row", "col"))
    return jax.shard_map(
        functools.partial(on_device, mesh.shape["grp"]),
        mesh=mesh, in_specs=in_specs, out_specs=out_specs, check_vma=False,
    )
```

```python
import functools

import jax
import jax.numpy as jnp
import numpy as np
from jax import lax
from jax.experimental import pallas as pl
from jax.experimental.pallas import tpu as pltpu
from jax.sharding import PartitionSpec as P

POLY = 4
CONSENSUS_WEIGHT = 1.0
MESH = pl.DeviceIdType.MESH

COMPS = 8
CHIPS = 16
HALF = CHIPS // 2
NEAR = 4


def smooth_basis(count):
    frequency = -1.0 + (2.0 * np.arange(count) + 1.0) / count
    factor = np.linalg.cholesky(np.linalg.inv(np.vander(frequency, POLY, True).T @ np.vander(frequency, POLY, True))[::-1, ::-1])
    return [[float(value) for value in row] for row in factor.T[::-1, ::-1]]


class Place:
    def __init__(self):
        row, col = lax.axis_index("row"), lax.axis_index("col")
        self.core = lax.rem(row, 2)
        self.chip = (row // 2) * NEAR + col

    def at(self, step):
        return lax.rem(self.chip + (step + CHIPS), CHIPS)

    def neighbour(self, step):
        chip = self.at(step)
        return {"row": (chip // NEAR) * 2 + self.core, "col": lax.rem(chip, NEAR)}

    def sibling(self):
        chip = self.chip
        return {"row": (chip // NEAR) * 2 + (1 - self.core), "col": lax.rem(chip, NEAR)}


def factors(real, imag):
    return real, imag - real, real + imag


def conjugate_turned(matrix):
    return [[factors(matrix[2 * col + row], -matrix[4 + 2 * col + row]) for col in range(2)] for row in range(2)]


def summed_parts(matrix):
    return [[(matrix[2 * row + col], matrix[4 + 2 * row + col], matrix[2 * row + col] + matrix[4 + 2 * row + col]) for col in range(2)] for row in range(2)]


def products(pairs, start=None):
    result = [None] * 8
    for row in range(2):
        for col in range(2):
            sums = [None] * 3
            for left_side, right_side, turned in pairs:
                for middle in range(2):
                    left, right = left_side[row][middle], right_side[middle][col]
                    (real, imag, both), (first, second, third) = (right, left) if turned else (left, right)
                    for n, term in enumerate((first * both, second * real, third * imag)):
                        sums[n] = term if sums[n] is None else sums[n] + term
            real, imag = sums[0] - sums[2], sums[0] + sums[1]
            if start is not None:
                real, imag = start[2 * row + col] + real, start[4 + 2 * row + col] + imag
            result[2 * row + col] = real
            result[4 + 2 * row + col] = imag
    return result


def split(value):
    high = value.astype(jnp.bfloat16)
    return high, (value - high.astype(jnp.float32)).astype(jnp.bfloat16)


def dot(left_side, right_side):
    return jnp.dot(left_side, right_side, preferred_element_type=jnp.float32)


ROWS = 16


REACH = 4
FAR = 4


def kernel(groups, gain_in, tan_in, order_in, flag_in, coh_in, out_ref,
           gain_ref, tan_ref, order_ref, flag_ref, coh_ref, all_ref, peer_buf, resid_ref,
           pick_ref, place_ref, mix_ref, gj_ref, left_ref, right_ref, row_ref, col_ref,
           part_ref, from_sib, total, far_buf, near_buf,
           in_sem, coh_sem, send_z, recv_z, send_s, recv_s, send_g, recv_g, send_w, recv_w, send_f, recv_f, send_n, recv_n):
    channels, comps, directions, tile_rows, tile_cols = coh_ref.shape
    stations = pick_ref.shape[1]
    values = comps * directions
    owned = gain_ref.shape[2]
    strips = tile_rows // ROWS
    place = Place()
    grp, row, col = lax.axis_index("grp"), lax.axis_index("row"), lax.axis_index("col")
    sibling = place.sibling()

    inputs = [
        pltpu.make_async_copy(source, target, in_sem.at[n])
        for n, (source, target) in enumerate(((gain_in, gain_ref), (tan_in, tan_ref), (order_in, order_ref), (flag_in, flag_ref)))
    ]
    for copy in inputs:
        copy.start()

    def peer(step):
        return {"grp": lax.rem(grp + (step + groups), groups)}

    partners = [place.neighbour(way * step) for step in range(1, max(REACH, FAR) + 1) for way in (1, -1)]
    partners = partners + [sibling] + [peer(step) for step in range(1, groups)]
    barrier = pltpu.get_barrier_semaphore()
    for device in partners:
        pl.semaphore_signal(barrier, inc=1, device_id=device, device_id_type=MESH)


    def block(channel, chip, core):
        start = pl.multiple_of(lax.rem(chip, NEAR) * owned, owned)
        return all_ref.at[channel, chip // NEAR, core, pl.ds(start, owned), :]

    def block_copy(channel, origin, core, target, send_sem, recv_sem):
        chip = place.at(origin)
        return pltpu.make_async_remote_copy(
            src_ref=block(channel, chip, core), dst_ref=block(channel, chip, core),
            send_sem=send_sem, recv_sem=recv_sem, device_id=target, device_id_type=MESH,
        )

    def limit(way):
        return HALF if way > 0 else HALF - 1

    def pass_on(channel, way, done):
        copies = []
        for step in range(REACH, 0, -1):
            if done + step <= limit(way):
                slot = HALF + way * (done + step)
                copies.append(block_copy(
                    channel, -way * done, place.core, place.neighbour(way * step), send_z.at[channel, slot], recv_z.at[channel, slot]
                ))
        return copies

    def to_sibling(channel, offset):
        slot = HALF + offset
        return block_copy(channel, -offset, place.core, sibling, send_s.at[channel, slot], recv_s.at[channel, slot])

    def from_ring(channel, offset):
        slot = HALF + offset
        return block_copy(channel, -offset, place.core, sibling, send_z.at[channel, slot], recv_z.at[channel, slot])

    def from_sibling(channel, offset):
        slot = HALF + offset
        return block_copy(channel, -offset, 1 - place.core, sibling, send_s.at[channel, slot], recv_s.at[channel, slot])

    offsets = range(1 - HALF, HALF + 1)
    stages = -(-HALF // REACH)

    def begin_gather(channel):
        for copy in pass_on(channel, 1, 0) + pass_on(channel, -1, 0) + [to_sibling(channel, 0)]:
            copy.start()

    def gather_stage(channel, stage):
        for distance in range(min((stage + 1) * REACH, HALF), stage * REACH, -1):
            for way in (1, -1):
                if distance <= limit(way):
                    from_ring(channel, way * distance).wait_recv()
                    if distance % REACH == 0:
                        for copy in pass_on(channel, way, distance):
                            copy.start()
                    to_sibling(channel, way * distance).start()

    def end_gather(channel):
        for offset in offsets:
            from_sibling(channel, offset).wait_recv()

    def to_peer(step):
        return pltpu.make_async_remote_copy(
            src_ref=peer_buf.at[0], dst_ref=peer_buf.at[step],
            send_sem=send_g.at[step], recv_sem=recv_g.at[step], device_id=peer(step), device_id_type=MESH,
        )

    def gather_sends(channel):
        copies = [to_sibling(channel, offset) for offset in offsets]
        for way in (1, -1):
            for done in range(0, limit(way), REACH):
                copies += pass_on(channel, way, done)
        return copies


    def rows_of(step):
        chip = place.at(step)
        return chip // NEAR, pl.ds(pl.multiple_of(lax.rem(chip, NEAR) * owned, owned), owned)

    def sums_for(channel, step):
        run, rows = rows_of(step)
        return total.at[channel, run, rows, :]

    def swap(channel):
        return pltpu.make_async_remote_copy(
            src_ref=part_ref.at[channel, :, 1 - place.core], dst_ref=from_sib.at[channel],
            send_sem=send_w.at[channel], recv_sem=recv_w.at[channel], device_id=sibling, device_id_type=MESH,
        )

    def hop(channel, source, buffer, slot, sends, recvs, step):
        return pltpu.make_async_remote_copy(
            src_ref=source, dst_ref=buffer.at[channel, slot], send_sem=sends.at[channel, slot], recv_sem=recvs.at[channel, slot],
            device_id=place.neighbour(step), device_id_type=MESH,
        )

    reaches = ((1, HALF - FAR), (-1, HALF - 1 - FAR))

    def to_add(channel):
        return {
            way * step: hop(channel, sums_for(channel, way * (step + FAR)), far_buf, FAR + way * step, send_f, recv_f, way * step)
            for way, most in reaches for step in range(most, 0, -1)
        }

    def direct(channel):
        return {
            way * step: hop(channel, sums_for(channel, way * step), near_buf, FAR + way * step, send_n, recv_n, way * step)
            for step in range(1, FAR) for way in (1, -1)
        }

    def added(channel):
        return {
            way * FAR: hop(channel, far_buf.at[channel, FAR if way > 0 else 2 * FAR + 1], near_buf, FAR + way * FAR, send_n, recv_n, way * FAR)
            for way in (1, -1)
        }

    def send_sums(channel):
        swap(channel).wait_recv()
        total[channel] = part_ref[channel, :, place.core] + from_sib[channel]
        for copy in list(to_add(channel).values()) + list(direct(channel).values()):
            copy.start()

    def send_added(channel):
        arrivals = to_add(channel)
        for (way, most), copy in zip(reaches, added(channel).values()):
            run, rows = rows_of(way * FAR)
            gathered = total[channel, run, rows, :]
            for step in range(1, most + 1):
                arrivals[way * step].wait_recv()
                gathered = gathered + far_buf[channel, FAR + way * step]
            far_buf[channel, FAR if way > 0 else 2 * FAR + 1] = gathered
            copy.start()

    def finish(channel):
        run, rows = rows_of(0)
        summed = total[channel, run, rows, :] + resid_ref[channel]
        for copy in list(direct(channel).values()) + list(added(channel).values()):
            copy.wait_recv()
        for slot in range(2 * FAR + 1):
            if slot != FAR:
                summed = summed + near_buf[channel, slot]
        out_ref[channel] = summed.T

    def sum_sends(channel):
        return [swap(channel)] + list(to_add(channel).values()) + list(direct(channel).values()) + list(added(channel).values())


    basis = smooth_basis(channels * groups)

    def heights(group, channel):
        frequency = (group * channels + channel).astype(jnp.float32) * (2.0 / (channels * groups)) + (1.0 / (channels * groups) - 1.0)
        powers = [1.0]
        for _ in range(1, POLY):
            powers.append(powers[-1] * frequency)
        return [sum(line[k] * powers[k] for k in range(POLY) if abs(line[k]) > 1e-9) for line in basis]

    def consensus():
        moments = [jnp.zeros((owned, values), jnp.float32) for _ in range(POLY)]
        for step in range(groups):
            if step > 0:
                to_peer(step).wait_recv()
            origin = lax.rem(grp + (groups - step), groups)
            for source in range(channels):
                seen = peer_buf[step, source]
                for k, height in enumerate(heights(origin, source)):
                    moments[k] = moments[k] + height * seen
        for channel in range(channels):
            smooth = sum(height * moment for height, moment in zip(heights(grp, channel), moments))
            resid_ref[channel] = CONSENSUS_WEIGHT * (peer_buf[0, channel] - smooth)


    lane = lax.broadcasted_iota(jnp.int32, (ROWS, 128), 1)
    same_row = (lane & (ROWS - 1)) == lax.broadcasted_iota(jnp.int32, (ROWS, 128), 0)

    def as_mask(hit):
        return hit.astype(jnp.float32).astype(jnp.bfloat16)

    def one_hots():
        col_ids = order_ref[pl.ds(col, 1), :]
        row_ids = order_ref[pl.ds(row // 2, 1), :]
        row_ids = jnp.where(lax.rem(row, 2) == 1, pltpu.roll(row_ids, tile_rows, 1), row_ids)
        for n, ids in enumerate((col_ids, row_ids)):
            ids = jnp.broadcast_to(ids, (128, 128))
            turned = ids.astype(jnp.float32).T.astype(jnp.int32)
            count = (tile_cols, tile_rows)[n]
            for tile in range(stations // 128):
                spot = lax.broadcasted_iota(jnp.int32, (128, 128), 1) + tile * 128
                pick_ref[n * tile_cols:n * tile_cols + count, tile * 128:(tile + 1) * 128] = as_mask(turned == spot)[:count]
                spot = lax.broadcasted_iota(jnp.int32, (128, 128), 0) + tile * 128
                place_ref[tile * 128:(tile + 1) * 128, n * 128:(n + 1) * 128] = as_mask(ids == spot)

    def prologue(channel):
        parts = split(all_ref[channel].reshape(stations, 2 * values))
        chosen = [dot(pick_ref[...], part) for part in parts]

        chosen_cols = chosen[0][:tile_cols] + chosen[1][:tile_cols]
        for array in range(2):
            turned = chosen_cols[:, array * values:(array + 1) * values].T.reshape(comps, directions, tile_cols)
            for line, entries in enumerate(conjugate_turned([turned[comp] for comp in range(comps)])):
                for end, entry in enumerate(entries):
                    for n, factor in enumerate(entry):
                        gj_ref[12 * array + 6 * line + 3 * end + n] = factor

        sides = [[
            one[tile_cols:, array * values:(array + 1) * values].T.reshape(comps, directions, tile_rows) for array in range(2)
        ] for one in chosen]
        for index in range(strips):
            lanes = slice(index * ROWS, (index + 1) * ROWS)
            for array in range(2):
                for line in range(2):
                    for part in range(2):
                        pieces = []
                        for side in sides:
                            for middle in range(2):
                                for other in range(2):
                                    value = side[array][4 * (part ^ other) + 2 * line + middle][:, lanes]
                                    pieces.append(-value if (part, other) == (0, 1) else value)
                        mix_ref[index, 4 * array + 2 * line + part] = jnp.concatenate(pieces, axis=1)
        col_ref[...] = jnp.zeros_like(col_ref)

    def strip(channel, index):
        rows = pl.ds(pl.multiple_of(index * ROWS, ROWS), ROWS)

        def forward(direction, change):
            here = slice(direction, direction + 1)
            coherent = [coh_ref[channel, comp, direction, rows, :] for comp in range(comps)]
            stacked = jnp.concatenate([
                jnp.concatenate([coherent[4 * part + 2 * middle], coherent[4 * part + 2 * middle + 1]], axis=1)
                for middle in range(2) for part in range(2)
            ], axis=0)
            mixing = jnp.concatenate([
                jnp.where(same_row, mix_ref[index, n, here, :], 0.0).astype(jnp.bfloat16) for n in range(8)
            ], axis=0)
            models = dot(mixing, jnp.concatenate([stacked, stacked], axis=0))

            def model(array):
                return [
                    models[ROWS * (4 * array + 2 * line + part):ROWS * (4 * array + 2 * line + part + 1), end * 128:(end + 1) * 128]
                    for part in range(2) for line in range(2) for end in range(2)
                ]

            model_left, tan_left = model(0), model(1)
            gain_j, tan_j = ([
                [[gj_ref[12 * array + 6 * line + 3 * end + n, here, :] for n in range(3)] for end in range(2)] for line in range(2)
            ] for array in range(2))
            for comp in range(comps):
                left_ref[comp, direction] = model_left[comp]
            model_right = products([(summed_parts([value.astype(jnp.float32) for value in coherent]), gain_j, False)])
            change = products([(summed_parts(tan_left), gain_j, False), (summed_parts(model_left), tan_j, False)], change)
            for part in range(2):
                for line in range(2):
                    for end in range(2):
                        for n, piece in enumerate(split(model_right[4 * part + 2 * line + end])):
                            lanes = slice((2 * n + end) * tile_cols, (2 * n + end + 1) * tile_cols)
                            right_ref[2 * line + part, direction, :, lanes] = piece
            return tuple(change)

        zero = jnp.zeros((ROWS, tile_cols), jnp.float32)
        change = (zero,) * comps
        for direction in range(directions):
            change = forward(direction, change)
        weight = flag_ref[rows, :].astype(jnp.float32)
        weighted = [value * weight for value in change]

        pieces = [split(value) for value in weighted]
        lines = [
            jnp.concatenate([
                jnp.concatenate([pieces[4 * part + 2 * line][n], pieces[4 * part + 2 * line + 1][n]], axis=1)
                for line in range(2) for part in range(2)
            ], axis=0) for n in range(2)
        ]
        lines = jnp.concatenate([
            jnp.concatenate([lines[0], lines[0]], axis=1), jnp.concatenate([lines[1], jnp.zeros_like(lines[1])], axis=1)
        ], axis=0)
        pairs = lax.dot_general(
            right_ref[...].reshape(4 * directions * ROWS, 4 * tile_cols), lines, (((1,), (1,)), ((), ())), preferred_element_type=jnp.float32
        ).reshape(4, directions, ROWS, 128)
        for n in range(4):
            row_ref[index, n] = jnp.sum(jnp.where(same_row[None], pairs[n], 0.0), axis=1)

        turned = conjugate_turned(weighted)
        for direction in range(directions):
            model_left = [left_ref[comp, direction] for comp in range(comps)]
            terms = products([(turned, summed_parts(model_left), True)])
            for comp in range(comps):
                folded = terms[comp][:8]
                for part in range(1, ROWS // 8):
                    folded = folded + terms[comp][8 * part:8 * part + 8]
                col_ref[comp, direction] += folded

    def epilogue(channel):
        sums = [[row_ref[index, n] for n in range(4)] for index in range(strips)]
        sums = [[value[:, :64] + value[:, 64:] for value in line] for line in sums]

        def cut(value, line, part):
            return value[:, (2 * line + part) * ROWS:(2 * line + part + 1) * ROWS]

        by_comp = []
        for part in range(2):
            for line in range(2):
                for end in range(2):
                    pieces = []
                    for value in sums:
                        if part == 0:
                            pieces.append(cut(value[2 * end], line, 0) + cut(value[2 * end + 1], line, 1))
                        else:
                            pieces.append(cut(value[2 * end], line, 1) - cut(value[2 * end + 1], line, 0))
                    by_comp.append(jnp.concatenate(pieces, axis=1))
        row_sums = jnp.concatenate(by_comp, axis=0)
        col_sums = jnp.sum(col_ref[...], axis=2).reshape(values, tile_cols)
        placed = jnp.zeros((stations, values), jnp.float32)
        for part in split(jnp.concatenate([col_sums, row_sums], axis=1)):
            placed = placed + lax.dot_general(
                place_ref[:, :tile_cols + tile_rows], part, (((1,), (1,)), ((), ())), preferred_element_type=jnp.float32
            )
        part_ref[channel] = placed.reshape(part_ref.shape[1:])
        swap(channel).start()


    inputs[0].wait()
    inputs[1].wait()
    own_start = pl.multiple_of(lax.rem(place.chip, NEAR) * owned, owned)
    for channel in range(channels):
        tan_t = tan_ref[channel].T
        peer_buf[0, channel] = tan_t
        own = all_ref.at[channel, place.chip // NEAR, place.core, pl.ds(own_start, owned), :]
        own[:, :values] = gain_ref[channel].T
        own[:, values:] = tan_t
    pl.semaphore_wait(barrier, len(partners))
    begin_gather(0)
    coherency = [pltpu.make_async_copy(coh_in.at[channel], coh_ref.at[channel], coh_sem.at[channel]) for channel in range(channels)]
    for copy in coherency:
        copy.start()
    inputs[2].wait()
    inputs[3].wait()
    one_hots()
    gather_stage(0, 0)
    begin_gather(1)
    for step in range(1, groups):
        to_peer(step).start()
    for stage in range(1, stages):
        gather_stage(0, stage)
    end_gather(0)
    for copy in coherency:
        copy.wait()

    def work(channel, _):
        @pl.when(channel == 1)
        def _():
            end_gather(1)

        prologue(channel)

        def one(index, _):
            for stage in range(stages):
                @pl.when(jnp.logical_and(channel == 0, index == stage))
                def _():
                    gather_stage(1, stage)

            @pl.when(jnp.logical_and(channel == 1, index == 0))
            def _():
                send_sums(0)

            @pl.when(jnp.logical_and(channel == 1, index == 3))
            def _():
                send_added(0)

            strip(channel, index)
            return 0

        lax.fori_loop(0, strips, one, 0)
        epilogue(channel)
        return 0

    lax.fori_loop(0, channels, work, 0)
    send_sums(1)
    consensus()
    finish(0)
    send_added(1)
    finish(1)
    for channel in range(channels):
        for copy in gather_sends(channel) + sum_sends(channel):
            copy.wait_send()
    for step in range(1, groups):
        to_peer(step).wait_send()


def on_device(groups, coherency, station_gains, tangent, flag_mask, station_order):
    channels, comps, directions, tile_rows, tile_cols = coherency.shape
    owned = tangent.shape[3]
    stations = station_order.shape[0]
    values = comps * directions
    runs = CHIPS // NEAR
    near = NEAR * owned
    strips = tile_rows // ROWS
    vmem = pltpu.VMEM
    f32, bf16 = jnp.float32, jnp.bfloat16

    def sems(*shape):
        return pltpu.SemaphoreType.DMA(shape)

    hbm = pl.BlockSpec(memory_space=pltpu.HBM)
    result = pl.pallas_call(
        functools.partial(kernel, groups),
        out_shape=jax.ShapeDtypeStruct((channels, values, owned), f32),
        in_specs=[hbm] * 5,
        out_specs=pl.BlockSpec(memory_space=pltpu.VMEM),
        scratch_shapes=[
            vmem((channels, values, owned), f32),
            vmem((channels, values, owned), f32),
            vmem((stations // 128, 128), jnp.int32),
            vmem((tile_rows, tile_cols), jnp.int32),
            vmem(coherency.shape, bf16),
            vmem((channels, runs, 2, near, 2 * values), f32),
            vmem((groups, channels, owned, values), f32),
            vmem((channels, owned, values), f32),
            vmem((tile_cols + tile_rows, stations), bf16),
            vmem((stations, 256), bf16),
            vmem((strips, comps, directions, 128), f32),
            vmem((24, directions, tile_cols), f32),
            vmem((comps, directions, ROWS, tile_cols), f32),
            vmem((4, directions, ROWS, 4 * tile_cols), bf16),
            vmem((strips, 4, directions, 128), f32),
            vmem((comps, directions, 8, tile_cols), f32),
            vmem((channels, runs, 2, near, values), f32),
            vmem((channels, runs, near, values), f32),
            vmem((channels, runs, near, values), f32),
            vmem((channels, 2 * FAR + 2, owned, values), f32),
            vmem((channels, 2 * FAR + 1, owned, values), f32),
            sems(4), sems(channels),
            sems(channels, CHIPS + 1), sems(channels, CHIPS + 1), sems(channels, CHIPS + 1), sems(channels, CHIPS + 1),
            sems(groups), sems(groups), sems(channels), sems(channels),
            sems(channels, 2 * FAR + 1), sems(channels, 2 * FAR + 1), sems(channels, 2 * FAR + 1), sems(channels, 2 * FAR + 1),
        ],
        compiler_params=pltpu.CompilerParams(collective_id=0, has_side_effects=True, vmem_limit_bytes=24 << 20),
        name="hessian",
    )(
        *(pltpu.with_memory_space_constraint(value, pltpu.HBM) for value in (
            station_gains.reshape(channels, values, owned),
            tangent.reshape(channels, values, owned),
            station_order.reshape(stations // 128, 128),
            flag_mask,
            coherency,
        ))
    )
    return result.reshape(channels, comps, directions, owned)


def solution(mesh):
    in_specs = (
        P("grp", None, None, "row", "col"),
        P("grp", None, None, ("row", "col")),
        P("grp", None, None, ("row", "col")),
        P("row", "col"),
        P(),
    )
    out_specs = P("grp", None, None, ("row", "col"))
    return jax.shard_map(
        functools.partial(on_device, mesh.shape["grp"]),
        mesh=mesh, in_specs=in_specs, out_specs=out_specs, check_vma=False,
    )
```

```python
import functools

import jax
import jax.numpy as jnp
import numpy as np
from jax import lax
from jax.experimental import pallas as pl
from jax.experimental.pallas import tpu as pltpu
from jax.sharding import PartitionSpec as P

POLY = 4
CONSENSUS_WEIGHT = 1.0
MESH = pl.DeviceIdType.MESH

COMPS = 8
CHIPS = 16
HALF = CHIPS // 2
NEAR = 4


def smooth_basis(count):
    frequency = -1.0 + (2.0 * np.arange(count) + 1.0) / count
    factor = np.linalg.cholesky(np.linalg.inv(np.vander(frequency, POLY, True).T @ np.vander(frequency, POLY, True))[::-1, ::-1])
    return [[float(value) for value in row] for row in factor.T[::-1, ::-1]]


class Place:
    def __init__(self):
        row, col = lax.axis_index("row"), lax.axis_index("col")
        self.core = lax.rem(row, 2)
        self.chip = (row // 2) * NEAR + col

    def at(self, step):
        return lax.rem(self.chip + (step + CHIPS), CHIPS)

    def neighbour(self, step):
        chip = self.at(step)
        return {"row": (chip // NEAR) * 2 + self.core, "col": lax.rem(chip, NEAR)}

    def sibling(self):
        chip = self.chip
        return {"row": (chip // NEAR) * 2 + (1 - self.core), "col": lax.rem(chip, NEAR)}


def factors(real, imag):
    return real, imag - real, real + imag


def conjugate_turned(matrix):
    return [[factors(matrix[2 * col + row], -matrix[4 + 2 * col + row]) for col in range(2)] for row in range(2)]


def summed_parts(matrix):
    return [[(matrix[2 * row + col], matrix[4 + 2 * row + col], matrix[2 * row + col] + matrix[4 + 2 * row + col]) for col in range(2)] for row in range(2)]


def products(pairs, start=None):
    result = [None] * 8
    for row in range(2):
        for col in range(2):
            sums = [None] * 3
            for left_side, right_side, turned in pairs:
                for middle in range(2):
                    left, right = left_side[row][middle], right_side[middle][col]
                    (real, imag, both), (first, second, third) = (right, left) if turned else (left, right)
                    for n, term in enumerate((first * both, second * real, third * imag)):
                        sums[n] = term if sums[n] is None else sums[n] + term
            real, imag = sums[0] - sums[2], sums[0] + sums[1]
            if start is not None:
                real, imag = start[2 * row + col] + real, start[4 + 2 * row + col] + imag
            result[2 * row + col] = real
            result[4 + 2 * row + col] = imag
    return result


def split(value):
    high = value.astype(jnp.bfloat16)
    return high, (value - high.astype(jnp.float32)).astype(jnp.bfloat16)


def dot(left_side, right_side):
    return jnp.dot(left_side, right_side, preferred_element_type=jnp.float32)


ROWS = 16


REACH = 4
FAR = 4


def kernel(groups, gain_in, tan_in, order_in, flag_in, coh_in, out_ref,
           gain_ref, tan_ref, order_ref, flag_ref, coh_ref, all_ref, peer_buf, resid_ref,
           pick_ref, place_ref, mix_ref, gj_ref, left_ref, right_ref, row_ref, col_ref,
           part_ref, from_sib, up_ref, down_ref, own_ref, near_up, near_down, far_up, added_ref, last_ref,
           in_sem, coh_sem, send_z, recv_z, send_s, recv_s, send_g, recv_g, send_w, recv_w, send_f, recv_f):
    channels, comps, directions, tile_rows, tile_cols = coh_ref.shape
    stations = pick_ref.shape[1]
    values = comps * directions
    owned = gain_ref.shape[2]
    strips = tile_rows // ROWS
    place = Place()
    grp, row, col = lax.axis_index("grp"), lax.axis_index("row"), lax.axis_index("col")
    sibling = place.sibling()

    inputs = [
        pltpu.make_async_copy(source, target, in_sem.at[n])
        for n, (source, target) in enumerate(((gain_in, gain_ref), (tan_in, tan_ref), (order_in, order_ref), (flag_in, flag_ref)))
    ]
    for copy in inputs:
        copy.start()

    def peer(step):
        return {"grp": lax.rem(grp + (step + groups), groups)}

    partners = [place.neighbour(way * step) for step in range(1, max(REACH, FAR) + 1) for way in (1, -1)]
    partners = partners + [sibling] + [peer(step) for step in range(1, groups)]
    barrier = pltpu.get_barrier_semaphore()
    for device in partners:
        pl.semaphore_signal(barrier, inc=1, device_id=device, device_id_type=MESH)


    def block(channel, chip, core):
        start = pl.multiple_of(lax.rem(chip, NEAR) * owned, owned)
        return all_ref.at[channel, chip // NEAR, core, pl.ds(start, owned), :]

    def block_copy(channel, origin, core, target, send_sem, recv_sem):
        chip = place.at(origin)
        return pltpu.make_async_remote_copy(
            src_ref=block(channel, chip, core), dst_ref=block(channel, chip, core),
            send_sem=send_sem, recv_sem=recv_sem, device_id=target, device_id_type=MESH,
        )

    def limit(way):
        return HALF if way > 0 else HALF - 1

    def pass_on(channel, way, done):
        copies = []
        for step in range(REACH, 0, -1):
            if done + step <= limit(way):
                slot = HALF + way * (done + step)
                copies.append(block_copy(
                    channel, -way * done, place.core, place.neighbour(way * step), send_z.at[channel, slot], recv_z.at[channel, slot]
                ))
        return copies

    def core_copy(channel, core):
        return pltpu.make_async_remote_copy(
            src_ref=all_ref.at[channel, :, core], dst_ref=all_ref.at[channel, :, core],
            send_sem=send_s.at[channel], recv_sem=recv_s.at[channel], device_id=sibling, device_id_type=MESH,
        )

    def from_ring(channel, offset):
        slot = HALF + offset
        return block_copy(channel, -offset, place.core, sibling, send_z.at[channel, slot], recv_z.at[channel, slot])

    stages = -(-HALF // REACH)

    def begin_gather(channel):
        for pair in zip(pass_on(channel, 1, 0), pass_on(channel, -1, 0)):
            for copy in pair:
                copy.start()

    def gather_stage(channel, stage):
        for distance in range(min((stage + 1) * REACH, HALF), stage * REACH, -1):
            for way in (1, -1):
                if distance <= limit(way):
                    from_ring(channel, way * distance).wait_recv()
                    if distance % REACH == 0:
                        for copy in pass_on(channel, way, distance):
                            copy.start()
        if stage == stages - 1:
            core_copy(channel, place.core).start()

    def end_gather(channel):
        core_copy(channel, 1 - place.core).wait_recv()

    def to_peer(step):
        return pltpu.make_async_remote_copy(
            src_ref=peer_buf.at[0], dst_ref=peer_buf.at[step],
            send_sem=send_g.at[step], recv_sem=recv_g.at[step], device_id=peer(step), device_id_type=MESH,
        )

    def gather_sends(channel):
        copies = [core_copy(channel, place.core)]
        for way in (1, -1):
            for done in range(0, limit(way), REACH):
                copies += pass_on(channel, way, done)
        return copies


    def rows_of(step):
        chip = place.at(step)
        return chip // NEAR, pl.ds(pl.multiple_of(lax.rem(chip, NEAR) * owned, owned), owned)

    def swap(channel):
        return pltpu.make_async_remote_copy(
            src_ref=part_ref.at[channel, :, 1 - place.core], dst_ref=from_sib.at[channel],
            send_sem=send_w.at[channel], recv_sem=recv_w.at[channel], device_id=sibling, device_id_type=MESH,
        )

    def hop(source, target, channel, index, step):
        return pltpu.make_async_remote_copy(
            src_ref=source, dst_ref=target, send_sem=send_f.at[channel, index], recv_sem=recv_f.at[channel, index],
            device_id=place.neighbour(step), device_id_type=MESH,
        )

    def first_hops(channel):
        copies = [hop(up_ref.at[channel, 1, FAR - 1], far_up.at[channel], channel, FAR - 1, FAR)]
        for n in reversed(range(FAR - 1)):
            copies.append(hop(up_ref.at[channel, :, n], near_up.at[channel, n], channel, n, n + 1))
            copies.append(hop(down_ref.at[channel, :, n], near_down.at[channel, n], channel, FAR + n, -1 - n))
        return copies

    def second_hops(channel):
        return [
            hop(added_ref.at[channel, n], last_ref.at[channel, n], channel, 2 * FAR - 1 + n, (1 - 2 * n) * FAR) for n in range(2)
        ]

    def send_sums(channel):
        swap(channel).wait_recv()
        for step in range(1 - HALF, HALF + 1):
            run, rows = rows_of(step)
            value = part_ref[channel, run, place.core, rows, :] + from_sib[channel, run, rows, :]
            if step == 0:
                own_ref[channel] = value
            else:
                side, distance = (up_ref, step - 1) if step > 0 else (down_ref, -step - 1)
                side[channel, distance // FAR, distance % FAR] = value
        for copy in first_hops(channel):
            copy.start()

    def send_added(channel):
        for copy in first_hops(channel):
            copy.wait_recv()
        up = up_ref[channel, 0, FAR - 1] + far_up[channel]
        down = down_ref[channel, 0, FAR - 1]
        for n in range(FAR - 1):
            up = up + near_up[channel, n, 1]
            down = down + near_down[channel, n, 1]
        added_ref[channel, 0] = up
        added_ref[channel, 1] = down
        for copy in second_hops(channel):
            copy.start()

    def finish(channel):
        summed = own_ref[channel] + resid_ref[channel]
        for n in range(FAR - 1):
            summed = summed + near_up[channel, n, 0] + near_down[channel, n, 0]
        for n, copy in enumerate(second_hops(channel)):
            copy.wait_recv()
            summed = summed + last_ref[channel, n]
        out_ref[channel] = summed.T

    def sum_sends(channel):
        return [swap(channel)] + first_hops(channel) + second_hops(channel)


    basis = smooth_basis(channels * groups)

    def heights(group, channel):
        frequency = (group * channels + channel).astype(jnp.float32) * (2.0 / (channels * groups)) + (1.0 / (channels * groups) - 1.0)
        powers = [1.0]
        for _ in range(1, POLY):
            powers.append(powers[-1] * frequency)
        return [sum(line[k] * powers[k] for k in range(POLY) if abs(line[k]) > 1e-9) for line in basis]

    def consensus():
        moments = [jnp.zeros((owned, values), jnp.float32) for _ in range(POLY)]
        for step in range(groups):
            if step > 0:
                to_peer(step).wait_recv()
            origin = lax.rem(grp + (groups - step), groups)
            for source in range(channels):
                seen = peer_buf[step, source]
                for k, height in enumerate(heights(origin, source)):
                    moments[k] = moments[k] + height * seen
        for channel in range(channels):
            smooth = sum(height * moment for height, moment in zip(heights(grp, channel), moments))
            resid_ref[channel] = CONSENSUS_WEIGHT * (peer_buf[0, channel] - smooth)


    lane = lax.broadcasted_iota(jnp.int32, (ROWS, 128), 1)
    same_row = (lane & (ROWS - 1)) == lax.broadcasted_iota(jnp.int32, (ROWS, 128), 0)

    def as_mask(hit):
        return hit.astype(jnp.float32).astype(jnp.bfloat16)

    def one_hots():
        col_ids = order_ref[pl.ds(col, 1), :]
        row_ids = order_ref[pl.ds(row // 2, 1), :]
        row_ids = jnp.where(lax.rem(row, 2) == 1, pltpu.roll(row_ids, tile_rows, 1), row_ids)
        for n, ids in enumerate((col_ids, row_ids)):
            ids = jnp.broadcast_to(ids, (128, 128))
            turned = ids.astype(jnp.float32).T.astype(jnp.int32)
            count = (tile_cols, tile_rows)[n]
            for tile in range(stations // 128):
                spot = lax.broadcasted_iota(jnp.int32, (128, 128), 1) + tile * 128
                pick_ref[n * tile_cols:n * tile_cols + count, tile * 128:(tile + 1) * 128] = as_mask(turned == spot)[:count]
                spot = lax.broadcasted_iota(jnp.int32, (128, 128), 0) + tile * 128
                place_ref[tile * 128:(tile + 1) * 128, n * 128:(n + 1) * 128] = as_mask(ids == spot)

    def prologue(channel):
        parts = split(all_ref[channel].reshape(stations, 2 * values))
        chosen = [dot(pick_ref[...], part) for part in parts]

        chosen_cols = chosen[0][:tile_cols] + chosen[1][:tile_cols]
        for array in range(2):
            turned = chosen_cols[:, array * values:(array + 1) * values].T.reshape(comps, directions, tile_cols)
            for line, entries in enumerate(conjugate_turned([turned[comp] for comp in range(comps)])):
                for end, entry in enumerate(entries):
                    for n, factor in enumerate(entry):
                        gj_ref[12 * array + 6 * line + 3 * end + n] = factor

        sides = [[
            one[tile_cols:, array * values:(array + 1) * values].T.reshape(comps, directions, tile_rows) for array in range(2)
        ] for one in chosen]
        for index in range(strips):
            lanes = slice(index * ROWS, (index + 1) * ROWS)
            for array in range(2):
                for line in range(2):
                    for part in range(2):
                        pieces = []
                        for side in sides:
                            for middle in range(2):
                                for other in range(2):
                                    value = side[array][4 * (part ^ other) + 2 * line + middle][:, lanes]
                                    pieces.append(-value if (part, other) == (0, 1) else value)
                        mix_ref[index, 4 * array + 2 * line + part] = jnp.concatenate(pieces, axis=1)
        col_ref[...] = jnp.zeros_like(col_ref)

    def strip(channel, index):
        rows = pl.ds(pl.multiple_of(index * ROWS, ROWS), ROWS)

        def forward(direction, change):
            here = slice(direction, direction + 1)
            coherent = [coh_ref[channel, comp, direction, rows, :] for comp in range(comps)]
            stacked = jnp.concatenate([
                jnp.concatenate([coherent[4 * part + 2 * middle], coherent[4 * part + 2 * middle + 1]], axis=1)
                for middle in range(2) for part in range(2)
            ], axis=0)
            mixing = jnp.concatenate([
                jnp.where(same_row, mix_ref[index, n, here, :], 0.0).astype(jnp.bfloat16) for n in range(8)
            ], axis=0)
            models = dot(mixing, jnp.concatenate([stacked, stacked], axis=0))

            def model(array):
                return [
                    models[ROWS * (4 * array + 2 * line + part):ROWS * (4 * array + 2 * line + part + 1), end * 128:(end + 1) * 128]
                    for part in range(2) for line in range(2) for end in range(2)
                ]

            model_left, tan_left = model(0), model(1)
            gain_j, tan_j = ([
                [[gj_ref[12 * array + 6 * line + 3 * end + n, here, :] for n in range(3)] for end in range(2)] for line in range(2)
            ] for array in range(2))
            for comp in range(comps):
                left_ref[comp, direction] = model_left[comp]
            model_right = products([(summed_parts([value.astype(jnp.float32) for value in coherent]), gain_j, False)])
            change = products([(summed_parts(tan_left), gain_j, False), (summed_parts(model_left), tan_j, False)], change)
            for part in range(2):
                for line in range(2):
                    for end in range(2):
                        for n, piece in enumerate(split(model_right[4 * part + 2 * line + end])):
                            lanes = slice((2 * n + end) * tile_cols, (2 * n + end + 1) * tile_cols)
                            right_ref[2 * line + part, direction, :, lanes] = piece
            return tuple(change)

        zero = jnp.zeros((ROWS, tile_cols), jnp.float32)
        change = (zero,) * comps
        for direction in range(directions):
            change = forward(direction, change)
        weight = flag_ref[rows, :].astype(jnp.float32)
        weighted = [value * weight for value in change]

        pieces = [split(value) for value in weighted]
        lines = [
            jnp.concatenate([
                jnp.concatenate([pieces[4 * part + 2 * line][n], pieces[4 * part + 2 * line + 1][n]], axis=1)
                for line in range(2) for part in range(2)
            ], axis=0) for n in range(2)
        ]
        lines = jnp.concatenate([
            jnp.concatenate([lines[0], lines[0]], axis=1), jnp.concatenate([lines[1], jnp.zeros_like(lines[1])], axis=1)
        ], axis=0)
        pairs = lax.dot_general(
            right_ref[...].reshape(4 * directions * ROWS, 4 * tile_cols), lines, (((1,), (1,)), ((), ())), preferred_element_type=jnp.float32
        ).reshape(4, directions, ROWS, 128)
        for n in range(4):
            row_ref[index, n] = jnp.sum(jnp.where(same_row[None], pairs[n], 0.0), axis=1)

        turned = conjugate_turned(weighted)
        for direction in range(directions):
            model_left = [left_ref[comp, direction] for comp in range(comps)]
            terms = products([(turned, summed_parts(model_left), True)])
            for comp in range(comps):
                folded = terms[comp][:8]
                for part in range(1, ROWS // 8):
                    folded = folded + terms[comp][8 * part:8 * part + 8]
                col_ref[comp, direction] += folded

    def epilogue(channel):
        sums = [[row_ref[index, n] for n in range(4)] for index in range(strips)]
        sums = [[value[:, :64] + value[:, 64:] for value in line] for line in sums]

        def cut(value, line, part):
            return value[:, (2 * line + part) * ROWS:(2 * line + part + 1) * ROWS]

        by_comp = []
        for part in range(2):
            for line in range(2):
                for end in range(2):
                    pieces = []
                    for value in sums:
                        if part == 0:
                            pieces.append(cut(value[2 * end], line, 0) + cut(value[2 * end + 1], line, 1))
                        else:
                            pieces.append(cut(value[2 * end], line, 1) - cut(value[2 * end + 1], line, 0))
                    by_comp.append(jnp.concatenate(pieces, axis=1))
        row_sums = jnp.concatenate(by_comp, axis=0)
        col_sums = jnp.sum(col_ref[...], axis=2).reshape(values, tile_cols)
        placed = jnp.zeros((stations, values), jnp.float32)
        for part in split(jnp.concatenate([col_sums, row_sums], axis=1)):
            placed = placed + lax.dot_general(
                place_ref[:, :tile_cols + tile_rows], part, (((1,), (1,)), ((), ())), preferred_element_type=jnp.float32
            )
        part_ref[channel] = placed.reshape(part_ref.shape[1:])
        swap(channel).start()


    inputs[0].wait()
    inputs[1].wait()
    own_start = pl.multiple_of(lax.rem(place.chip, NEAR) * owned, owned)
    for channel in range(channels):
        tan_t = tan_ref[channel].T
        peer_buf[0, channel] = tan_t
        own = all_ref.at[channel, place.chip // NEAR, place.core, pl.ds(own_start, owned), :]
        own[:, :values] = gain_ref[channel].T
        own[:, values:] = tan_t
    pl.semaphore_wait(barrier, len(partners))
    begin_gather(0)
    coherency = [pltpu.make_async_copy(coh_in.at[channel], coh_ref.at[channel], coh_sem.at[channel]) for channel in range(channels)]
    for copy in coherency:
        copy.start()
    inputs[2].wait()
    inputs[3].wait()
    one_hots()
    gather_stage(0, 0)
    begin_gather(1)
    for stage in range(1, stages):
        gather_stage(0, stage)
    for step in range(1, groups):
        to_peer(step).start()
    end_gather(0)
    for copy in coherency:
        copy.wait()

    def work(channel, _):
        @pl.when(channel == 1)
        def _():
            end_gather(1)

        prologue(channel)

        def one(index, _):
            for stage in range(stages):
                @pl.when(jnp.logical_and(channel == 0, index == 2 * stage))
                def _():
                    gather_stage(1, stage)

            @pl.when(jnp.logical_and(channel == 1, index == 1))
            def _():
                send_sums(0)

            @pl.when(jnp.logical_and(channel == 1, index == 3))
            def _():
                send_added(0)

            strip(channel, index)
            return 0

        lax.fori_loop(0, strips, one, 0)
        epilogue(channel)
        return 0

    lax.fori_loop(0, channels, work, 0)
    send_sums(1)
    consensus()
    finish(0)
    for copy in gather_sends(0) + gather_sends(1) + [to_peer(step) for step in range(1, groups)] + sum_sends(0):
        copy.wait_send()
    send_added(1)
    finish(1)
    for copy in sum_sends(1):
        copy.wait_send()


def on_device(groups, coherency, station_gains, tangent, flag_mask, station_order):
    channels, comps, directions, tile_rows, tile_cols = coherency.shape
    owned = tangent.shape[3]
    stations = station_order.shape[0]
    values = comps * directions
    runs = CHIPS // NEAR
    near = NEAR * owned
    strips = tile_rows // ROWS
    vmem = pltpu.VMEM
    f32, bf16 = jnp.float32, jnp.bfloat16

    def sems(*shape):
        return pltpu.SemaphoreType.DMA(shape)

    hbm = pl.BlockSpec(memory_space=pltpu.HBM)
    result = pl.pallas_call(
        functools.partial(kernel, groups),
        out_shape=jax.ShapeDtypeStruct((channels, values, owned), f32),
        in_specs=[hbm] * 5,
        out_specs=pl.BlockSpec(memory_space=pltpu.VMEM),
        scratch_shapes=[
            vmem((channels, values, owned), f32),
            vmem((channels, values, owned), f32),
            vmem((stations // 128, 128), jnp.int32),
            vmem((tile_rows, tile_cols), jnp.int32),
            vmem(coherency.shape, bf16),
            vmem((channels, runs, 2, near, 2 * values), f32),
            vmem((groups, channels, owned, values), f32),
            vmem((channels, owned, values), f32),
            vmem((tile_cols + tile_rows, stations), bf16),
            vmem((stations, 256), bf16),
            vmem((strips, comps, directions, 128), f32),
            vmem((24, directions, tile_cols), f32),
            vmem((comps, directions, ROWS, tile_cols), f32),
            vmem((4, directions, ROWS, 4 * tile_cols), bf16),
            vmem((strips, 4, directions, 128), f32),
            vmem((comps, directions, 8, tile_cols), f32),
            vmem((channels, runs, 2, near, values), f32),
            vmem((channels, runs, near, values), f32),
            vmem((channels, 2, FAR, owned, values), f32),
            vmem((channels, 2, FAR, owned, values), f32),
            vmem((channels, owned, values), f32),
            vmem((channels, FAR - 1, 2, owned, values), f32),
            vmem((channels, FAR - 1, 2, owned, values), f32),
            vmem((channels, owned, values), f32),
            vmem((channels, 2, owned, values), f32),
            vmem((channels, 2, owned, values), f32),
            sems(4), sems(channels),
            sems(channels, CHIPS + 1), sems(channels, CHIPS + 1), sems(channels), sems(channels),
            sems(groups), sems(groups), sems(channels), sems(channels),
            sems(channels, 2 * FAR + 1), sems(channels, 2 * FAR + 1),
        ],
        compiler_params=pltpu.CompilerParams(collective_id=0, has_side_effects=True, vmem_limit_bytes=24 << 20),
        name="hessian",
    )(
        *(pltpu.with_memory_space_constraint(value, pltpu.HBM) for value in (
            station_gains.reshape(channels, values, owned),
            tangent.reshape(channels, values, owned),
            station_order.reshape(stations // 128, 128),
            flag_mask,
            coherency,
        ))
    )
    return result.reshape(channels, comps, directions, owned)


def solution(mesh):
    in_specs = (
        P("grp", None, None, "row", "col"),
        P("grp", None, None, ("row", "col")),
        P("grp", None, None, ("row", "col")),
        P("row", "col"),
        P(),
    )
    out_specs = P("grp", None, None, ("row", "col"))
    return jax.shard_map(
        functools.partial(on_device, mesh.shape["grp"]),
        mesh=mesh, in_specs=in_specs, out_specs=out_specs, check_vma=False,
    )
```

```python
import functools

import jax
import jax.numpy as jnp
import numpy as np
from jax import lax
from jax.experimental import pallas as pl
from jax.experimental.pallas import tpu as pltpu
from jax.sharding import PartitionSpec as P

POLY = 4
CONSENSUS_WEIGHT = 1.0
MESH = pl.DeviceIdType.MESH

COMPS = 8
CHIPS = 16
HALF = CHIPS // 2
NEAR = 4


def smooth_basis(count):
    frequency = -1.0 + (2.0 * np.arange(count) + 1.0) / count
    factor = np.linalg.cholesky(np.linalg.inv(np.vander(frequency, POLY, True).T @ np.vander(frequency, POLY, True))[::-1, ::-1])
    return [[float(value) for value in row] for row in factor.T[::-1, ::-1]]


class Place:
    def __init__(self):
        row, col = lax.axis_index("row"), lax.axis_index("col")
        self.core = lax.rem(row, 2)
        self.chip = (row // 2) * NEAR + col

    def at(self, step):
        return lax.rem(self.chip + (step + CHIPS), CHIPS)

    def neighbour(self, step):
        chip = self.at(step)
        return {"row": (chip // NEAR) * 2 + self.core, "col": lax.rem(chip, NEAR)}

    def sibling(self):
        chip = self.chip
        return {"row": (chip // NEAR) * 2 + (1 - self.core), "col": lax.rem(chip, NEAR)}


def factors(real, imag):
    return real, imag - real, real + imag


def conjugate_turned(matrix):
    return [[factors(matrix[2 * col + row], -matrix[4 + 2 * col + row]) for col in range(2)] for row in range(2)]


def summed_parts(matrix):
    return [[(matrix[2 * row + col], matrix[4 + 2 * row + col], matrix[2 * row + col] + matrix[4 + 2 * row + col]) for col in range(2)] for row in range(2)]


def products(pairs, start=None):
    result = [None] * 8
    for row in range(2):
        for col in range(2):
            sums = [None] * 3
            for left_side, right_side, turned in pairs:
                for middle in range(2):
                    left, right = left_side[row][middle], right_side[middle][col]
                    (real, imag, both), (first, second, third) = (right, left) if turned else (left, right)
                    for n, term in enumerate((first * both, second * real, third * imag)):
                        sums[n] = term if sums[n] is None else sums[n] + term
            real, imag = sums[0] - sums[2], sums[0] + sums[1]
            if start is not None:
                real, imag = start[2 * row + col] + real, start[4 + 2 * row + col] + imag
            result[2 * row + col] = real
            result[4 + 2 * row + col] = imag
    return result


def split(value):
    high = value.astype(jnp.bfloat16)
    return high, (value - high.astype(jnp.float32)).astype(jnp.bfloat16)


def dot(left_side, right_side):
    return jnp.dot(left_side, right_side, preferred_element_type=jnp.float32)


ROWS = 16


REACH = 4
FAR = 4


def kernel(groups, gain_in, tan_in, order_in, flag_in, coh_in, out_ref,
           gain_ref, tan_ref, order_ref, flag_ref, coh_ref, all_ref, peer_buf, resid_ref,
           pick_ref, place_ref, chosen_ref, mix_ref, gj_ref, left_ref, right_ref, row_ref, col_ref,
           part_ref, from_sib, up_ref, down_ref, own_ref, near_up, near_down, far_up, added_ref, last_ref,
           in_sem, coh_sem, send_z, recv_z, send_s, recv_s, send_g, recv_g, send_w, recv_w, send_f, recv_f):
    channels, comps, directions, tile_rows, tile_cols = coh_ref.shape
    stations = 2 * pick_ref.shape[2]
    near = place_ref.shape[2]
    values = comps * directions
    owned = gain_ref.shape[2]
    strips = tile_rows // ROWS
    place = Place()
    grp, row, col = lax.axis_index("grp"), lax.axis_index("row"), lax.axis_index("col")
    sibling = place.sibling()

    inputs = [
        pltpu.make_async_copy(source, target, in_sem.at[n])
        for n, (source, target) in enumerate(((gain_in, gain_ref), (tan_in, tan_ref), (order_in, order_ref), (flag_in, flag_ref)))
    ]
    for copy in inputs:
        copy.start()

    def peer(step):
        return {"grp": lax.rem(grp + (step + groups), groups)}

    partners = [place.neighbour(way * step) for step in range(1, max(REACH, FAR) + 1) for way in (1, -1)]
    partners = partners + [sibling] + [peer(step) for step in range(1, groups)]
    barrier = pltpu.get_barrier_semaphore()
    for device in partners:
        pl.semaphore_signal(barrier, inc=1, device_id=device, device_id_type=MESH)


    def block(channel, chip, core):
        start = pl.multiple_of(lax.rem(chip, NEAR) * owned, owned)
        return all_ref.at[channel, chip // NEAR, core, pl.ds(start, owned), :]

    def block_copy(channel, origin, core, target, send_sem, recv_sem):
        chip = place.at(origin)
        return pltpu.make_async_remote_copy(
            src_ref=block(channel, chip, core), dst_ref=block(channel, chip, core),
            send_sem=send_sem, recv_sem=recv_sem, device_id=target, device_id_type=MESH,
        )

    def limit(way):
        return HALF if way > 0 else HALF - 1

    def pass_on(channel, way, done):
        copies = []
        for step in range(REACH, 0, -1):
            if done + step <= limit(way):
                slot = HALF + way * (done + step)
                copies.append(block_copy(
                    channel, -way * done, place.core, place.neighbour(way * step), send_z.at[channel, slot], recv_z.at[channel, slot]
                ))
        return copies

    def core_copy(channel, core):
        return pltpu.make_async_remote_copy(
            src_ref=all_ref.at[channel, :, core], dst_ref=all_ref.at[channel, :, core],
            send_sem=send_s.at[channel], recv_sem=recv_s.at[channel], device_id=sibling, device_id_type=MESH,
        )

    def from_ring(channel, offset):
        slot = HALF + offset
        return block_copy(channel, -offset, place.core, sibling, send_z.at[channel, slot], recv_z.at[channel, slot])

    stages = -(-HALF // REACH)

    def begin_gather(channel):
        for pair in zip(pass_on(channel, 1, 0), pass_on(channel, -1, 0)):
            for copy in pair:
                copy.start()

    def gather_stage(channel, stage):
        for distance in range(min((stage + 1) * REACH, HALF), stage * REACH, -1):
            for way in (1, -1):
                if distance <= limit(way):
                    from_ring(channel, way * distance).wait_recv()
                    if distance % REACH == 0:
                        for copy in pass_on(channel, way, distance):
                            copy.start()
        if stage == stages - 1:
            core_copy(channel, place.core).start()

    def end_gather(channel):
        core_copy(channel, 1 - place.core).wait_recv()

    def to_peer(step):
        return pltpu.make_async_remote_copy(
            src_ref=peer_buf.at[0], dst_ref=peer_buf.at[step],
            send_sem=send_g.at[step], recv_sem=recv_g.at[step], device_id=peer(step), device_id_type=MESH,
        )

    def gather_sends(channel):
        copies = [core_copy(channel, place.core)]
        for way in (1, -1):
            for done in range(0, limit(way), REACH):
                copies += pass_on(channel, way, done)
        return copies


    def rows_of(step):
        chip = place.at(step)
        return chip // NEAR, pl.ds(pl.multiple_of(lax.rem(chip, NEAR) * owned, owned), owned)

    def swap(channel):
        return pltpu.make_async_remote_copy(
            src_ref=part_ref.at[channel, :, 1 - place.core], dst_ref=from_sib.at[channel],
            send_sem=send_w.at[channel], recv_sem=recv_w.at[channel], device_id=sibling, device_id_type=MESH,
        )

    def hop(source, target, channel, index, step):
        return pltpu.make_async_remote_copy(
            src_ref=source, dst_ref=target, send_sem=send_f.at[channel, index], recv_sem=recv_f.at[channel, index],
            device_id=place.neighbour(step), device_id_type=MESH,
        )

    def first_hops(channel):
        copies = [hop(up_ref.at[channel, 1, FAR - 1], far_up.at[channel], channel, FAR - 1, FAR)]
        for n in reversed(range(FAR - 1)):
            copies.append(hop(up_ref.at[channel, :, n], near_up.at[channel, n], channel, n, n + 1))
            copies.append(hop(down_ref.at[channel, :, n], near_down.at[channel, n], channel, FAR + n, -1 - n))
        return copies

    def second_hops(channel):
        return [
            hop(added_ref.at[channel, n], last_ref.at[channel, n], channel, 2 * FAR - 1 + n, (1 - 2 * n) * FAR) for n in range(2)
        ]

    def send_sums(channel):
        swap(channel).wait_recv()
        for step in range(1 - HALF, HALF + 1):
            run, rows = rows_of(step)
            value = part_ref[channel, run, place.core, rows, :] + from_sib[channel, run, rows, :]
            if step == 0:
                own_ref[channel] = value
            else:
                side, distance = (up_ref, step - 1) if step > 0 else (down_ref, -step - 1)
                side[channel, distance // FAR, distance % FAR] = value
        for copy in first_hops(channel):
            copy.start()

    def send_added(channel):
        for copy in first_hops(channel):
            copy.wait_recv()
        up = up_ref[channel, 0, FAR - 1] + far_up[channel]
        down = down_ref[channel, 0, FAR - 1]
        for n in range(FAR - 1):
            up = up + near_up[channel, n, 1]
            down = down + near_down[channel, n, 1]
        added_ref[channel, 0] = up
        added_ref[channel, 1] = down
        for copy in second_hops(channel):
            copy.start()

    def finish(channel):
        summed = own_ref[channel] + resid_ref[channel]
        for n in range(FAR - 1):
            summed = summed + near_up[channel, n, 0] + near_down[channel, n, 0]
        for n, copy in enumerate(second_hops(channel)):
            copy.wait_recv()
            summed = summed + last_ref[channel, n]
        out_ref[channel] = summed.T

    def sum_sends(channel):
        return [swap(channel)] + first_hops(channel) + second_hops(channel)


    basis = smooth_basis(channels * groups)

    def heights(group, channel):
        frequency = (group * channels + channel).astype(jnp.float32) * (2.0 / (channels * groups)) + (1.0 / (channels * groups) - 1.0)
        powers = [1.0]
        for _ in range(1, POLY):
            powers.append(powers[-1] * frequency)
        return [sum(line[k] * powers[k] for k in range(POLY) if abs(line[k]) > 1e-9) for line in basis]

    def consensus():
        moments = [jnp.zeros((owned, values), jnp.float32) for _ in range(POLY)]
        for step in range(groups):
            if step > 0:
                to_peer(step).wait_recv()
            origin = lax.rem(grp + (groups - step), groups)
            for source in range(channels):
                seen = peer_buf[step, source]
                for k, height in enumerate(heights(origin, source)):
                    moments[k] = moments[k] + height * seen
        for channel in range(channels):
            smooth = sum(height * moment for height, moment in zip(heights(grp, channel), moments))
            resid_ref[channel] = CONSENSUS_WEIGHT * (peer_buf[0, channel] - smooth)


    lane = lax.broadcasted_iota(jnp.int32, (ROWS, 128), 1)
    same_row = (lane & (ROWS - 1)) == lax.broadcasted_iota(jnp.int32, (ROWS, 128), 0)

    def as_mask(hit):
        return hit.astype(jnp.float32).astype(jnp.bfloat16)

    def one_hots():
        col_ids = order_ref[pl.ds(col, 1), :]
        row_ids = order_ref[pl.ds(row // 2, 1), :]
        row_ids = jnp.where(lax.rem(row, 2) == 1, pltpu.roll(row_ids, tile_rows, 1), row_ids)
        for n, ids in enumerate((col_ids, row_ids)):
            ids = jnp.broadcast_to(ids, (128, 128))
            turned = ids.astype(jnp.float32).T.astype(jnp.int32)
            count = (tile_cols, tile_rows)[n]
            for tile in range(stations // 128):
                spot = lax.broadcasted_iota(jnp.int32, (128, 128), 0) + tile * 128
                place_ref[tile, :, :, n * 128:(n + 1) * 128] = as_mask(ids == spot).reshape(2, near, 128)
            for core in range(2):
                for tile in range(stations // 256):
                    lane_in_core = lax.broadcasted_iota(jnp.int32, (128, 128), 1) + tile * 128
                    spot = (lane_in_core // near) * (2 * near) + core * near + lane_in_core % near
                    pick_ref[core, n * tile_cols:n * tile_cols + count, tile * 128:(tile + 1) * 128] = as_mask(turned == spot)[:count]

    def chosen_from(channel, core):
        held = all_ref[channel, :, core].reshape(stations // 2, 2 * values)
        return [dot(pick_ref[core], part) for part in split(held)]

    def choose_own(channel):
        for n, value in enumerate(chosen_from(channel, place.core)):
            chosen_ref[n] = value

    def prologue(channel):
        chosen = [chosen_ref[n] + value for n, value in enumerate(chosen_from(channel, 1 - place.core))]

        chosen_cols = chosen[0][:tile_cols] + chosen[1][:tile_cols]
        for array in range(2):
            turned = chosen_cols[:, array * values:(array + 1) * values].T.reshape(comps, directions, tile_cols)
            for line, entries in enumerate(conjugate_turned([turned[comp] for comp in range(comps)])):
                for end, entry in enumerate(entries):
                    for n, factor in enumerate(entry):
                        gj_ref[12 * array + 6 * line + 3 * end + n] = factor

        sides = [[
            one[tile_cols:, array * values:(array + 1) * values].T.reshape(comps, directions, tile_rows) for array in range(2)
        ] for one in chosen]
        for index in range(strips):
            lanes = slice(index * ROWS, (index + 1) * ROWS)
            for array in range(2):
                for line in range(2):
                    for part in range(2):
                        pieces = []
                        for side in sides:
                            for middle in range(2):
                                for other in range(2):
                                    value = side[array][4 * (part ^ other) + 2 * line + middle][:, lanes]
                                    pieces.append(-value if (part, other) == (0, 1) else value)
                        mix_ref[index, 4 * array + 2 * line + part] = jnp.concatenate(pieces, axis=1)
        col_ref[...] = jnp.zeros_like(col_ref)

    def strip(channel, index):
        rows = pl.ds(pl.multiple_of(index * ROWS, ROWS), ROWS)

        def forward(direction, change):
            here = slice(direction, direction + 1)
            coherent = [coh_ref[channel, comp, direction, rows, :] for comp in range(comps)]
            stacked = jnp.concatenate([
                jnp.concatenate([coherent[4 * part + 2 * middle], coherent[4 * part + 2 * middle + 1]], axis=1)
                for middle in range(2) for part in range(2)
            ], axis=0)
            mixing = jnp.concatenate([
                jnp.where(same_row, mix_ref[index, n, here, :], 0.0).astype(jnp.bfloat16) for n in range(8)
            ], axis=0)
            models = dot(mixing, jnp.concatenate([stacked, stacked], axis=0))

            def model(array):
                return [
                    models[ROWS * (4 * array + 2 * line + part):ROWS * (4 * array + 2 * line + part + 1), end * 128:(end + 1) * 128]
                    for part in range(2) for line in range(2) for end in range(2)
                ]

            model_left, tan_left = model(0), model(1)
            gain_j, tan_j = ([
                [[gj_ref[12 * array + 6 * line + 3 * end + n, here, :] for n in range(3)] for end in range(2)] for line in range(2)
            ] for array in range(2))
            for comp in range(comps):
                left_ref[comp, direction] = model_left[comp]
            model_right = products([(summed_parts([value.astype(jnp.float32) for value in coherent]), gain_j, False)])
            change = products([(summed_parts(tan_left), gain_j, False), (summed_parts(model_left), tan_j, False)], change)
            for part in range(2):
                for line in range(2):
                    for end in range(2):
                        for n, piece in enumerate(split(model_right[4 * part + 2 * line + end])):
                            lanes = slice((2 * n + end) * tile_cols, (2 * n + end + 1) * tile_cols)
                            right_ref[2 * line + part, direction, :, lanes] = piece
            return tuple(change)

        zero = jnp.zeros((ROWS, tile_cols), jnp.float32)
        change = (zero,) * comps
        for direction in range(directions):
            change = forward(direction, change)
        weight = flag_ref[rows, :].astype(jnp.float32)
        weighted = [value * weight for value in change]

        pieces = [split(value) for value in weighted]
        lines = [
            jnp.concatenate([
                jnp.concatenate([pieces[4 * part + 2 * line][n], pieces[4 * part + 2 * line + 1][n]], axis=1)
                for line in range(2) for part in range(2)
            ], axis=0) for n in range(2)
        ]
        lines = jnp.concatenate([
            jnp.concatenate([lines[0], lines[0]], axis=1), jnp.concatenate([lines[1], jnp.zeros_like(lines[1])], axis=1)
        ], axis=0)
        pairs = lax.dot_general(
            right_ref[...].reshape(4 * directions * ROWS, 4 * tile_cols), lines, (((1,), (1,)), ((), ())), preferred_element_type=jnp.float32
        ).reshape(4, directions, ROWS, 128)
        for n in range(4):
            row_ref[index, n] = jnp.sum(jnp.where(same_row[None], pairs[n], 0.0), axis=1)

        turned = conjugate_turned(weighted)
        for direction in range(directions):
            model_left = [left_ref[comp, direction] for comp in range(comps)]
            terms = products([(turned, summed_parts(model_left), True)])
            for comp in range(comps):
                folded = terms[comp][:8]
                for part in range(1, ROWS // 8):
                    folded = folded + terms[comp][8 * part:8 * part + 8]
                col_ref[comp, direction] += folded

    def epilogue(channel):
        sums = [[row_ref[index, n] for n in range(4)] for index in range(strips)]
        sums = [[value[:, :64] + value[:, 64:] for value in line] for line in sums]

        def cut(value, line, part):
            return value[:, (2 * line + part) * ROWS:(2 * line + part + 1) * ROWS]

        by_comp = []
        for part in range(2):
            for line in range(2):
                for end in range(2):
                    pieces = []
                    for value in sums:
                        if part == 0:
                            pieces.append(cut(value[2 * end], line, 0) + cut(value[2 * end + 1], line, 1))
                        else:
                            pieces.append(cut(value[2 * end], line, 1) - cut(value[2 * end + 1], line, 0))
                    by_comp.append(jnp.concatenate(pieces, axis=1))
        row_sums = jnp.concatenate(by_comp, axis=0)
        col_sums = jnp.sum(col_ref[...], axis=2).reshape(values, tile_cols)
        parts = split(jnp.concatenate([col_sums, row_sums], axis=1))

        def put(core):
            spots = place_ref[:, core].reshape(stations // 2, 256)[:, :tile_cols + tile_rows]
            placed = sum(lax.dot_general(spots, part, (((1,), (1,)), ((), ())), preferred_element_type=jnp.float32) for part in parts)
            part_ref[channel, :, core] = placed.reshape(stations // (2 * near), near, values)

        put(1 - place.core)
        swap(channel).start()
        put(place.core)


    inputs[0].wait()
    inputs[1].wait()
    own_start = pl.multiple_of(lax.rem(place.chip, NEAR) * owned, owned)
    for channel in range(channels):
        tan_t = tan_ref[channel].T
        peer_buf[0, channel] = tan_t
        own = all_ref.at[channel, place.chip // NEAR, place.core, pl.ds(own_start, owned), :]
        own[:, :values] = gain_ref[channel].T
        own[:, values:] = tan_t
    pl.semaphore_wait(barrier, len(partners))
    begin_gather(0)
    coherency = [pltpu.make_async_copy(coh_in.at[channel], coh_ref.at[channel], coh_sem.at[channel]) for channel in range(channels)]
    for copy in coherency:
        copy.start()
    inputs[2].wait()
    inputs[3].wait()
    one_hots()
    gather_stage(0, 0)
    begin_gather(1)
    for stage in range(1, stages):
        gather_stage(0, stage)
    for step in range(1, groups):
        to_peer(step).start()
    for copy in coherency:
        copy.wait()

    def work(channel, _):
        choose_own(channel)
        for ready in range(channels):
            @pl.when(channel == ready)
            def _():
                end_gather(ready)

        prologue(channel)

        def one(index, _):
            for stage in range(stages):
                @pl.when(jnp.logical_and(channel == 0, index == 2 * stage))
                def _():
                    gather_stage(1, stage)

            @pl.when(jnp.logical_and(channel == 1, index == 1))
            def _():
                send_sums(0)

            @pl.when(jnp.logical_and(channel == 1, index == 3))
            def _():
                send_added(0)

            strip(channel, index)
            return 0

        lax.fori_loop(0, strips, one, 0)
        epilogue(channel)
        return 0

    lax.fori_loop(0, channels, work, 0)
    send_sums(1)
    consensus()
    finish(0)
    for copy in gather_sends(0) + gather_sends(1) + [to_peer(step) for step in range(1, groups)] + sum_sends(0):
        copy.wait_send()
    send_added(1)
    finish(1)
    for copy in sum_sends(1):
        copy.wait_send()


def on_device(groups, coherency, station_gains, tangent, flag_mask, station_order):
    channels, comps, directions, tile_rows, tile_cols = coherency.shape
    owned = tangent.shape[3]
    stations = station_order.shape[0]
    values = comps * directions
    runs = CHIPS // NEAR
    near = NEAR * owned
    strips = tile_rows // ROWS
    vmem = pltpu.VMEM
    f32, bf16 = jnp.float32, jnp.bfloat16

    def sems(*shape):
        return pltpu.SemaphoreType.DMA(shape)

    hbm = pl.BlockSpec(memory_space=pltpu.HBM)
    result = pl.pallas_call(
        functools.partial(kernel, groups),
        out_shape=jax.ShapeDtypeStruct((channels, values, owned), f32),
        in_specs=[hbm] * 5,
        out_specs=pl.BlockSpec(memory_space=pltpu.VMEM),
        scratch_shapes=[
            vmem((channels, values, owned), f32),
            vmem((channels, values, owned), f32),
            vmem((stations // 128, 128), jnp.int32),
            vmem((tile_rows, tile_cols), jnp.int32),
            vmem(coherency.shape, bf16),
            vmem((channels, runs, 2, near, 2 * values), f32),
            vmem((groups, channels, owned, values), f32),
            vmem((channels, owned, values), f32),
            vmem((2, tile_cols + tile_rows, stations // 2), bf16),
            vmem((runs, 2, near, 256), bf16),
            vmem((2, tile_cols + tile_rows, 2 * values), f32),
            vmem((strips, comps, directions, 128), f32),
            vmem((24, directions, tile_cols), f32),
            vmem((comps, directions, ROWS, tile_cols), f32),
            vmem((4, directions, ROWS, 4 * tile_cols), bf16),
            vmem((strips, 4, directions, 128), f32),
            vmem((comps, directions, 8, tile_cols), f32),
            vmem((channels, runs, 2, near, values), f32),
            vmem((channels, runs, near, values), f32),
            vmem((channels, 2, FAR, owned, values), f32),
            vmem((channels, 2, FAR, owned, values), f32),
            vmem((channels, owned, values), f32),
            vmem((channels, FAR - 1, 2, owned, values), f32),
            vmem((channels, FAR - 1, 2, owned, values), f32),
            vmem((channels, owned, values), f32),
            vmem((channels, 2, owned, values), f32),
            vmem((channels, 2, owned, values), f32),
            sems(4), sems(channels),
            sems(channels, CHIPS + 1), sems(channels, CHIPS + 1), sems(channels), sems(channels),
            sems(groups), sems(groups), sems(channels), sems(channels),
            sems(channels, 2 * FAR + 1), sems(channels, 2 * FAR + 1),
        ],
        compiler_params=pltpu.CompilerParams(collective_id=0, has_side_effects=True, vmem_limit_bytes=24 << 20),
        name="hessian",
    )(
        *(pltpu.with_memory_space_constraint(value, pltpu.HBM) for value in (
            station_gains.reshape(channels, values, owned),
            tangent.reshape(channels, values, owned),
            station_order.reshape(stations // 128, 128),
            flag_mask,
            coherency,
        ))
    )
    return result.reshape(channels, comps, directions, owned)


def solution(mesh):
    in_specs = (
        P("grp", None, None, "row", "col"),
        P("grp", None, None, ("row", "col")),
        P("grp", None, None, ("row", "col")),
        P("row", "col"),
        P(),
    )
    out_specs = P("grp", None, None, ("row", "col"))
    return jax.shard_map(
        functools.partial(on_device, mesh.shape["grp"]),
        mesh=mesh, in_specs=in_specs, out_specs=out_specs, check_vma=False,
    )
```

```python
import functools

import jax
import jax.numpy as jnp
import numpy as np
from jax import lax
from jax.experimental import pallas as pl
from jax.experimental.pallas import tpu as pltpu
from jax.sharding import PartitionSpec as P

POLY = 4
CONSENSUS_WEIGHT = 1.0
MESH = pl.DeviceIdType.MESH

COMPS = 8
CHIPS = 16
HALF = CHIPS // 2
NEAR = 4


def smooth_basis(count):
    frequency = -1.0 + (2.0 * np.arange(count) + 1.0) / count
    factor = np.linalg.cholesky(np.linalg.inv(np.vander(frequency, POLY, True).T @ np.vander(frequency, POLY, True))[::-1, ::-1])
    return [[float(value) for value in row] for row in factor.T[::-1, ::-1]]


class Place:
    def __init__(self):
        row, col = lax.axis_index("row"), lax.axis_index("col")
        self.core = lax.rem(row, 2)
        self.chip = (row // 2) * NEAR + col

    def at(self, step):
        return lax.rem(self.chip + (step + CHIPS), CHIPS)

    def neighbour(self, step):
        chip = self.at(step)
        return {"row": (chip // NEAR) * 2 + self.core, "col": lax.rem(chip, NEAR)}

    def sibling(self):
        chip = self.chip
        return {"row": (chip // NEAR) * 2 + (1 - self.core), "col": lax.rem(chip, NEAR)}


def factors(real, imag):
    return real, imag - real, real + imag


def conjugate_turned(matrix):
    return [[factors(matrix[2 * col + row], -matrix[4 + 2 * col + row]) for col in range(2)] for row in range(2)]


def summed_parts(matrix):
    return [[(matrix[2 * row + col], matrix[4 + 2 * row + col], matrix[2 * row + col] + matrix[4 + 2 * row + col]) for col in range(2)] for row in range(2)]


def products(pairs, start=None):
    result = [None] * 8
    for row in range(2):
        for col in range(2):
            sums = [None] * 3
            for left_side, right_side, turned in pairs:
                for middle in range(2):
                    left, right = left_side[row][middle], right_side[middle][col]
                    (real, imag, both), (first, second, third) = (right, left) if turned else (left, right)
                    for n, term in enumerate((first * both, second * real, third * imag)):
                        sums[n] = term if sums[n] is None else sums[n] + term
            real, imag = sums[0] - sums[2], sums[0] + sums[1]
            if start is not None:
                real, imag = start[2 * row + col] + real, start[4 + 2 * row + col] + imag
            result[2 * row + col] = real
            result[4 + 2 * row + col] = imag
    return result


def split(value):
    high = value.astype(jnp.bfloat16)
    return high, (value - high.astype(jnp.float32)).astype(jnp.bfloat16)


def dot(left_side, right_side):
    return jnp.dot(left_side, right_side, preferred_element_type=jnp.float32)


ROWS = 16


REACH = 4
FAR = 4


def kernel(groups, gain_in, tan_in, order_in, flag_in, coh_in, out_ref,
           gain_ref, tan_ref, order_ref, flag_ref, coh_ref, all_ref, peer_buf, resid_ref,
           pick_ref, place_ref, chosen_ref, mix_ref, gj_ref, left_ref, right_ref, row_ref, col_ref,
           part_ref, from_sib, up_ref, down_ref, own_ref, near_up, near_down, far_up, added_ref, last_ref,
           in_sem, coh_sem, send_z, recv_z, send_s, recv_s, send_g, recv_g, send_w, recv_w, send_f, recv_f):
    channels, comps, directions, tile_rows, tile_cols = coh_ref.shape
    stations = 2 * pick_ref.shape[2]
    near = place_ref.shape[2]
    values = comps * directions
    owned = gain_ref.shape[2]
    strips = tile_rows // ROWS
    place = Place()
    grp, row, col = lax.axis_index("grp"), lax.axis_index("row"), lax.axis_index("col")
    sibling = place.sibling()

    inputs = [
        pltpu.make_async_copy(source, target, in_sem.at[n])
        for n, (source, target) in enumerate(((gain_in, gain_ref), (tan_in, tan_ref), (order_in, order_ref), (flag_in, flag_ref)))
    ]
    for copy in inputs:
        copy.start()

    def peer(step):
        return {"grp": lax.rem(grp + (step + groups), groups)}

    partners = [place.neighbour(way * step) for step in range(1, max(REACH, FAR) + 1) for way in (1, -1)]
    partners = partners + [sibling] + [peer(step) for step in range(1, groups)]
    barrier = pltpu.get_barrier_semaphore()
    for device in partners:
        pl.semaphore_signal(barrier, inc=1, device_id=device, device_id_type=MESH)


    def block(channel, chip, core):
        start = pl.multiple_of(lax.rem(chip, NEAR) * owned, owned)
        return all_ref.at[channel, chip // NEAR, core, pl.ds(start, owned), :]

    def block_copy(channel, origin, core, target, send_sem, recv_sem):
        chip = place.at(origin)
        return pltpu.make_async_remote_copy(
            src_ref=block(channel, chip, core), dst_ref=block(channel, chip, core),
            send_sem=send_sem, recv_sem=recv_sem, device_id=target, device_id_type=MESH,
        )

    def limit(way):
        return HALF if way > 0 else HALF - 1

    def pass_on(channel, way, done):
        copies = []
        for step in range(REACH, 0, -1):
            if done + step <= limit(way):
                slot = HALF + way * (done + step)
                copies.append(block_copy(
                    channel, -way * done, place.core, place.neighbour(way * step), send_z.at[channel, slot], recv_z.at[channel, slot]
                ))
        return copies

    def core_copy(channel, core):
        return pltpu.make_async_remote_copy(
            src_ref=all_ref.at[channel, :, core], dst_ref=all_ref.at[channel, :, core],
            send_sem=send_s.at[channel], recv_sem=recv_s.at[channel], device_id=sibling, device_id_type=MESH,
        )

    def from_ring(channel, offset):
        slot = HALF + offset
        return block_copy(channel, -offset, place.core, sibling, send_z.at[channel, slot], recv_z.at[channel, slot])

    stages = -(-HALF // REACH)

    def begin_gather(channel):
        for pair in zip(pass_on(channel, 1, 0), pass_on(channel, -1, 0)):
            for copy in pair:
                copy.start()

    def gather_stage(channel, stage):
        for distance in range(min((stage + 1) * REACH, HALF), stage * REACH, -1):
            for way in (1, -1):
                if distance <= limit(way):
                    from_ring(channel, way * distance).wait_recv()
                    if distance % REACH == 0:
                        for copy in pass_on(channel, way, distance):
                            copy.start()
        if stage == stages - 1:
            core_copy(channel, place.core).start()

    def end_gather(channel):
        core_copy(channel, 1 - place.core).wait_recv()

    def to_peer(step):
        return pltpu.make_async_remote_copy(
            src_ref=peer_buf.at[0], dst_ref=peer_buf.at[step],
            send_sem=send_g.at[step], recv_sem=recv_g.at[step], device_id=peer(step), device_id_type=MESH,
        )

    def gather_sends(channel):
        copies = [core_copy(channel, place.core)]
        for way in (1, -1):
            for done in range(0, limit(way), REACH):
                copies += pass_on(channel, way, done)
        return copies


    def rows_of(step):
        chip = place.at(step)
        return chip // NEAR, pl.ds(pl.multiple_of(lax.rem(chip, NEAR) * owned, owned), owned)

    def swap(channel):
        return pltpu.make_async_remote_copy(
            src_ref=part_ref.at[channel, :, 1 - place.core], dst_ref=from_sib.at[channel],
            send_sem=send_w.at[channel], recv_sem=recv_w.at[channel], device_id=sibling, device_id_type=MESH,
        )

    def hop(source, target, channel, index, step):
        return pltpu.make_async_remote_copy(
            src_ref=source, dst_ref=target, send_sem=send_f.at[channel, index], recv_sem=recv_f.at[channel, index],
            device_id=place.neighbour(step), device_id_type=MESH,
        )

    def first_hops(channel):
        copies = [hop(up_ref.at[channel, 1, FAR - 1], far_up.at[channel], channel, FAR - 1, FAR)]
        for n in reversed(range(FAR - 1)):
            copies.append(hop(up_ref.at[channel, :, n], near_up.at[channel, n], channel, n, n + 1))
            copies.append(hop(down_ref.at[channel, :, n], near_down.at[channel, n], channel, FAR + n, -1 - n))
        return copies

    def second_hops(channel):
        return [
            hop(added_ref.at[channel, n], last_ref.at[channel, n], channel, 2 * FAR - 1 + n, (1 - 2 * n) * FAR) for n in range(2)
        ]

    def send_sums(channel):
        swap(channel).wait_recv()
        for step in range(1 - HALF, HALF + 1):
            run, rows = rows_of(step)
            value = part_ref[channel, run, place.core, rows, :] + from_sib[channel, run, rows, :]
            if step == 0:
                own_ref[channel] = value
            else:
                side, distance = (up_ref, step - 1) if step > 0 else (down_ref, -step - 1)
                side[channel, distance // FAR, distance % FAR] = value
        for copy in first_hops(channel):
            copy.start()

    def send_added(channel):
        for copy in first_hops(channel):
            copy.wait_recv()
        up = up_ref[channel, 0, FAR - 1] + far_up[channel]
        down = down_ref[channel, 0, FAR - 1]
        for n in range(FAR - 1):
            up = up + near_up[channel, n, 1]
            down = down + near_down[channel, n, 1]
        added_ref[channel, 0] = up
        added_ref[channel, 1] = down
        for copy in second_hops(channel):
            copy.start()

    def finish(channel):
        summed = own_ref[channel] + resid_ref[channel]
        for n in range(FAR - 1):
            summed = summed + near_up[channel, n, 0] + near_down[channel, n, 0]
        for n, copy in enumerate(second_hops(channel)):
            copy.wait_recv()
            summed = summed + last_ref[channel, n]
        out_ref[channel] = summed.T

    def sum_sends(channel):
        return [swap(channel)] + first_hops(channel) + second_hops(channel)


    basis = smooth_basis(channels * groups)

    def heights(group, channel):
        frequency = (group * channels + channel).astype(jnp.float32) * (2.0 / (channels * groups)) + (1.0 / (channels * groups) - 1.0)
        powers = [1.0]
        for _ in range(1, POLY):
            powers.append(powers[-1] * frequency)
        return [sum(line[k] * powers[k] for k in range(POLY) if abs(line[k]) > 1e-9) for line in basis]

    def consensus():
        moments = [jnp.zeros((owned, values), jnp.float32) for _ in range(POLY)]
        for step in range(groups):
            if step > 0:
                to_peer(step).wait_recv()
            origin = lax.rem(grp + (groups - step), groups)
            for source in range(channels):
                seen = peer_buf[step, source]
                for k, height in enumerate(heights(origin, source)):
                    moments[k] = moments[k] + height * seen
        for channel in range(channels):
            smooth = sum(height * moment for height, moment in zip(heights(grp, channel), moments))
            resid_ref[channel] = CONSENSUS_WEIGHT * (peer_buf[0, channel] - smooth)


    lane = lax.broadcasted_iota(jnp.int32, (ROWS, 128), 1)
    same_row = (lane & (ROWS - 1)) == lax.broadcasted_iota(jnp.int32, (ROWS, 128), 0)

    def as_mask(hit):
        return hit.astype(jnp.float32).astype(jnp.bfloat16)

    def one_hots():
        col_ids = order_ref[pl.ds(col, 1), :]
        row_ids = order_ref[pl.ds(row // 2, 1), :]
        row_ids = jnp.where(lax.rem(row, 2) == 1, pltpu.roll(row_ids, tile_rows, 1), row_ids)
        for n, ids in enumerate((col_ids, row_ids)):
            ids = jnp.broadcast_to(ids, (128, 128))
            turned = ids.astype(jnp.float32).T.astype(jnp.int32)
            count = (tile_cols, tile_rows)[n]
            for tile in range(stations // 128):
                spot = lax.broadcasted_iota(jnp.int32, (128, 128), 0) + tile * 128
                place_ref[tile, :, :, n * 128:(n + 1) * 128] = as_mask(ids == spot).reshape(2, near, 128)
            for core in range(2):
                for tile in range(stations // 256):
                    lane_in_core = lax.broadcasted_iota(jnp.int32, (128, 128), 1) + tile * 128
                    spot = (lane_in_core // near) * (2 * near) + core * near + lane_in_core % near
                    pick_ref[core, n * tile_cols:n * tile_cols + count, tile * 128:(tile + 1) * 128] = as_mask(turned == spot)[:count]

    def chosen_from(channel, core):
        held = all_ref[channel, :, core].reshape(stations // 2, 2 * values)
        return [dot(pick_ref[core], part) for part in split(held)]

    def choose_own(channel):
        for n, value in enumerate(chosen_from(channel, place.core)):
            chosen_ref[n] = value

    def prologue(channel):
        chosen = [chosen_ref[n] + value for n, value in enumerate(chosen_from(channel, 1 - place.core))]

        chosen_cols = chosen[0][:tile_cols] + chosen[1][:tile_cols]
        for array in range(2):
            turned = chosen_cols[:, array * values:(array + 1) * values].T.reshape(comps, directions, tile_cols)
            for line, entries in enumerate(conjugate_turned([turned[comp] for comp in range(comps)])):
                for end, entry in enumerate(entries):
                    for n, factor in enumerate(entry):
                        gj_ref[12 * array + 6 * line + 3 * end + n] = factor

        sides = [[
            one[tile_cols:, array * values:(array + 1) * values].T.reshape(comps, directions, tile_rows) for array in range(2)
        ] for one in chosen]
        for index in range(strips):
            lanes = slice(index * ROWS, (index + 1) * ROWS)
            for array in range(2):
                for line in range(2):
                    for part in range(2):
                        pieces = []
                        for side in sides:
                            for middle in range(2):
                                for other in range(2):
                                    value = side[array][4 * (part ^ other) + 2 * line + middle][:, lanes]
                                    pieces.append(-value if (part, other) == (0, 1) else value)
                        mix_ref[index, 4 * array + 2 * line + part] = jnp.concatenate(pieces, axis=1)
        col_ref[...] = jnp.zeros_like(col_ref)

    def strip(channel, index):
        rows = pl.ds(pl.multiple_of(index * ROWS, ROWS), ROWS)

        def forward(direction, change):
            here = slice(direction, direction + 1)
            coherent = [coh_ref[channel, comp, direction, rows, :] for comp in range(comps)]
            stacked = jnp.concatenate([
                jnp.concatenate([coherent[4 * part + 2 * middle], coherent[4 * part + 2 * middle + 1]], axis=1)
                for middle in range(2) for part in range(2)
            ], axis=0)
            mixing = jnp.concatenate([
                jnp.where(same_row, mix_ref[index, n, here, :], 0.0).astype(jnp.bfloat16) for n in range(8)
            ], axis=0)
            models = dot(mixing, jnp.concatenate([stacked, stacked], axis=0))

            def model(array):
                return [
                    models[ROWS * (4 * array + 2 * line + part):ROWS * (4 * array + 2 * line + part + 1), end * 128:(end + 1) * 128]
                    for part in range(2) for line in range(2) for end in range(2)
                ]

            model_left, tan_left = model(0), model(1)
            gain_j, tan_j = ([
                [[gj_ref[12 * array + 6 * line + 3 * end + n, here, :] for n in range(3)] for end in range(2)] for line in range(2)
            ] for array in range(2))
            for comp in range(comps):
                left_ref[comp, direction] = model_left[comp]
            model_right = products([(summed_parts([value.astype(jnp.float32) for value in coherent]), gain_j, False)])
            change = products([(summed_parts(tan_left), gain_j, False), (summed_parts(model_left), tan_j, False)], change)
            for part in range(2):
                for line in range(2):
                    for end in range(2):
                        for n, piece in enumerate(split(model_right[4 * part + 2 * line + end])):
                            lanes = slice((2 * n + end) * tile_cols, (2 * n + end + 1) * tile_cols)
                            right_ref[2 * line + part, direction, :, lanes] = piece
            return tuple(change)

        zero = jnp.zeros((ROWS, tile_cols), jnp.float32)
        change = (zero,) * comps
        for direction in range(directions):
            change = forward(direction, change)
        weight = flag_ref[rows, :].astype(jnp.float32)
        weighted = [value * weight for value in change]

        pieces = [split(value) for value in weighted]
        lines = [
            jnp.concatenate([
                jnp.concatenate([pieces[4 * part + 2 * line][n], pieces[4 * part + 2 * line + 1][n]], axis=1)
                for line in range(2) for part in range(2)
            ], axis=0) for n in range(2)
        ]
        lines = jnp.concatenate([
            jnp.concatenate([lines[0], lines[0]], axis=1), jnp.concatenate([lines[1], jnp.zeros_like(lines[1])], axis=1)
        ], axis=0)
        pairs = lax.dot_general(
            right_ref[...].reshape(4 * directions * ROWS, 4 * tile_cols), lines, (((1,), (1,)), ((), ())), preferred_element_type=jnp.float32
        ).reshape(4, directions, ROWS, 128)
        for n in range(4):
            row_ref[index, n] = jnp.sum(jnp.where(same_row[None], pairs[n], 0.0), axis=1)

        turned = conjugate_turned(weighted)
        for direction in range(directions):
            model_left = [left_ref[comp, direction] for comp in range(comps)]
            terms = products([(turned, summed_parts(model_left), True)])
            for comp in range(comps):
                folded = terms[comp][:8]
                for part in range(1, ROWS // 8):
                    folded = folded + terms[comp][8 * part:8 * part + 8]
                col_ref[comp, direction] += folded

    def epilogue(channel):
        sums = [[row_ref[index, n] for n in range(4)] for index in range(strips)]
        sums = [[value[:, :64] + value[:, 64:] for value in line] for line in sums]

        def cut(value, line, part):
            return value[:, (2 * line + part) * ROWS:(2 * line + part + 1) * ROWS]

        by_comp = []
        for part in range(2):
            for line in range(2):
                for end in range(2):
                    pieces = []
                    for value in sums:
                        if part == 0:
                            pieces.append(cut(value[2 * end], line, 0) + cut(value[2 * end + 1], line, 1))
                        else:
                            pieces.append(cut(value[2 * end], line, 1) - cut(value[2 * end + 1], line, 0))
                    by_comp.append(jnp.concatenate(pieces, axis=1))
        row_sums = jnp.concatenate(by_comp, axis=0)
        col_sums = jnp.sum(col_ref[...], axis=2).reshape(values, tile_cols)
        parts = split(jnp.concatenate([col_sums, row_sums], axis=1))

        def put(core):
            spots = place_ref[:, core].reshape(stations // 2, 256)[:, :tile_cols + tile_rows]
            placed = sum(lax.dot_general(spots, part, (((1,), (1,)), ((), ())), preferred_element_type=jnp.float32) for part in parts)
            part_ref[channel, :, core] = placed.reshape(stations // (2 * near), near, values)

        put(1 - place.core)
        swap(channel).start()
        put(place.core)


    inputs[0].wait()
    inputs[1].wait()
    own_start = pl.multiple_of(lax.rem(place.chip, NEAR) * owned, owned)
    for channel in range(channels):
        tan_t = tan_ref[channel].T
        peer_buf[0, channel] = tan_t
        own = all_ref.at[channel, place.chip // NEAR, place.core, pl.ds(own_start, owned), :]
        own[:, :values] = gain_ref[channel].T
        own[:, values:] = tan_t
    pl.semaphore_wait(barrier, len(partners))
    begin_gather(0)
    coherency = [pltpu.make_async_copy(coh_in.at[channel], coh_ref.at[channel], coh_sem.at[channel]) for channel in range(channels)]
    for copy in coherency:
        copy.start()
    inputs[2].wait()
    inputs[3].wait()
    one_hots()
    gather_stage(0, 0)
    begin_gather(1)
    for stage in range(1, stages):
        gather_stage(0, stage)
    for step in range(1, groups):
        to_peer(step).start()
    for copy in coherency:
        copy.wait()

    def work(channel, _):
        choose_own(channel)
        for ready in range(channels):
            @pl.when(channel == ready)
            def _():
                end_gather(ready)

        prologue(channel)

        def one(index, _):
            for stage in range(stages):
                @pl.when(jnp.logical_and(channel == 0, index == (strips - 1) * stage // (stages - 1)))
                def _():
                    gather_stage(1, stage)

            @pl.when(jnp.logical_and(channel == 1, index == 1))
            def _():
                send_sums(0)

            strip(channel, index)
            return 0

        lax.fori_loop(0, strips, one, 0)
        epilogue(channel)
        return 0

    lax.fori_loop(0, channels, work, 0)
    send_sums(1)
    send_added(0)
    consensus()
    for copy in gather_sends(0) + gather_sends(1) + [to_peer(step) for step in range(1, groups)]:
        copy.wait_send()
    send_added(1)
    finish(0)
    for copy in sum_sends(0):
        copy.wait_send()
    finish(1)
    for copy in sum_sends(1):
        copy.wait_send()


def on_device(groups, coherency, station_gains, tangent, flag_mask, station_order):
    channels, comps, directions, tile_rows, tile_cols = coherency.shape
    owned = tangent.shape[3]
    stations = station_order.shape[0]
    values = comps * directions
    runs = CHIPS // NEAR
    near = NEAR * owned
    strips = tile_rows // ROWS
    vmem = pltpu.VMEM
    f32, bf16 = jnp.float32, jnp.bfloat16

    def sems(*shape):
        return pltpu.SemaphoreType.DMA(shape)

    hbm = pl.BlockSpec(memory_space=pltpu.HBM)
    result = pl.pallas_call(
        functools.partial(kernel, groups),
        out_shape=jax.ShapeDtypeStruct((channels, values, owned), f32),
        in_specs=[hbm] * 5,
        out_specs=pl.BlockSpec(memory_space=pltpu.VMEM),
        scratch_shapes=[
            vmem((channels, values, owned), f32),
            vmem((channels, values, owned), f32),
            vmem((stations // 128, 128), jnp.int32),
            vmem((tile_rows, tile_cols), jnp.int32),
            vmem(coherency.shape, bf16),
            vmem((channels, runs, 2, near, 2 * values), f32),
            vmem((groups, channels, owned, values), f32),
            vmem((channels, owned, values), f32),
            vmem((2, tile_cols + tile_rows, stations // 2), bf16),
            vmem((runs, 2, near, 256), bf16),
            vmem((2, tile_cols + tile_rows, 2 * values), f32),
            vmem((strips, comps, directions, 128), f32),
            vmem((24, directions, tile_cols), f32),
            vmem((comps, directions, ROWS, tile_cols), f32),
            vmem((4, directions, ROWS, 4 * tile_cols), bf16),
            vmem((strips, 4, directions, 128), f32),
            vmem((comps, directions, 8, tile_cols), f32),
            vmem((channels, runs, 2, near, values), f32),
            vmem((channels, runs, near, values), f32),
            vmem((channels, 2, FAR, owned, values), f32),
            vmem((channels, 2, FAR, owned, values), f32),
            vmem((channels, owned, values), f32),
            vmem((channels, FAR - 1, 2, owned, values), f32),
            vmem((channels, FAR - 1, 2, owned, values), f32),
            vmem((channels, owned, values), f32),
            vmem((channels, 2, owned, values), f32),
            vmem((channels, 2, owned, values), f32),
            sems(4), sems(channels),
            sems(channels, CHIPS + 1), sems(channels, CHIPS + 1), sems(channels), sems(channels),
            sems(groups), sems(groups), sems(channels), sems(channels),
            sems(channels, 2 * FAR + 1), sems(channels, 2 * FAR + 1),
        ],
        compiler_params=pltpu.CompilerParams(collective_id=0, has_side_effects=True, vmem_limit_bytes=24 << 20),
        name="hessian",
    )(
        *(pltpu.with_memory_space_constraint(value, pltpu.HBM) for value in (
            station_gains.reshape(channels, values, owned),
            tangent.reshape(channels, values, owned),
            station_order.reshape(stations // 128, 128),
            flag_mask,
            coherency,
        ))
    )
    return result.reshape(channels, comps, directions, owned)


def solution(mesh):
    in_specs = (
        P("grp", None, None, "row", "col"),
        P("grp", None, None, ("row", "col")),
        P("grp", None, None, ("row", "col")),
        P("row", "col"),
        P(),
    )
    out_specs = P("grp", None, None, ("row", "col"))
    return jax.shard_map(
        functools.partial(on_device, mesh.shape["grp"]),
        mesh=mesh, in_specs=in_specs, out_specs=out_specs, check_vma=False,
    )
```

```python
import functools

import jax
import jax.numpy as jnp
import numpy as np
from jax import lax
from jax.experimental import pallas as pl
from jax.experimental.pallas import tpu as pltpu
from jax.sharding import PartitionSpec as P

POLY = 4
CONSENSUS_WEIGHT = 1.0
MESH = pl.DeviceIdType.MESH

COMPS = 8
CHIPS = 16
HALF = CHIPS // 2
NEAR = 4


def smooth_basis(count):
    frequency = -1.0 + (2.0 * np.arange(count) + 1.0) / count
    factor = np.linalg.cholesky(np.linalg.inv(np.vander(frequency, POLY, True).T @ np.vander(frequency, POLY, True))[::-1, ::-1])
    return [[float(value) for value in row] for row in factor.T[::-1, ::-1]]


class Place:
    def __init__(self):
        row, col = lax.axis_index("row"), lax.axis_index("col")
        self.core = lax.rem(row, 2)
        self.chip = (row // 2) * NEAR + col

    def at(self, step):
        return lax.rem(self.chip + (step + CHIPS), CHIPS)

    def neighbour(self, step):
        chip = self.at(step)
        return {"row": (chip // NEAR) * 2 + self.core, "col": lax.rem(chip, NEAR)}

    def sibling(self):
        chip = self.chip
        return {"row": (chip // NEAR) * 2 + (1 - self.core), "col": lax.rem(chip, NEAR)}


def factors(real, imag):
    return real, imag - real, real + imag


def conjugate_turned(matrix):
    return [[factors(matrix[2 * col + row], -matrix[4 + 2 * col + row]) for col in range(2)] for row in range(2)]


def summed_parts(matrix):
    return [[(matrix[2 * row + col], matrix[4 + 2 * row + col], matrix[2 * row + col] + matrix[4 + 2 * row + col]) for col in range(2)] for row in range(2)]


def products(pairs, start=None):
    result = [None] * 8
    for row in range(2):
        for col in range(2):
            sums = [None] * 3
            for left_side, right_side, turned in pairs:
                for middle in range(2):
                    left, right = left_side[row][middle], right_side[middle][col]
                    (real, imag, both), (first, second, third) = (right, left) if turned else (left, right)
                    for n, term in enumerate((first * both, second * real, third * imag)):
                        sums[n] = term if sums[n] is None else sums[n] + term
            real, imag = sums[0] - sums[2], sums[0] + sums[1]
            if start is not None:
                real, imag = start[2 * row + col] + real, start[4 + 2 * row + col] + imag
            result[2 * row + col] = real
            result[4 + 2 * row + col] = imag
    return result


def split(value):
    high = value.astype(jnp.bfloat16)
    return high, (value - high.astype(jnp.float32)).astype(jnp.bfloat16)


def dot(left_side, right_side):
    return jnp.dot(left_side, right_side, preferred_element_type=jnp.float32)


ROWS = 16


REACH = (3, 4)
FAR = 4


def kernel(groups, gain_in, tan_in, order_in, flag_in, coh_in, out_ref,
           gain_ref, tan_ref, order_ref, flag_ref, coh_ref, all_ref, peer_buf, resid_ref,
           pick_ref, place_ref, chosen_ref, mix_ref, gj_ref, left_ref, right_ref, row_ref, col_ref,
           part_ref, from_sib, up_ref, down_ref, own_ref, near_up, near_down, far_up, added_ref, last_ref,
           in_sem, coh_sem, send_z, recv_z, send_s, recv_s, send_g, recv_g, send_w, recv_w, send_f, recv_f):
    channels, comps, directions, tile_rows, tile_cols = coh_ref.shape
    stations = 2 * pick_ref.shape[2]
    near = place_ref.shape[2]
    values = comps * directions
    owned = gain_ref.shape[2]
    strips = tile_rows // ROWS
    place = Place()
    grp, row, col = lax.axis_index("grp"), lax.axis_index("row"), lax.axis_index("col")
    sibling = place.sibling()

    inputs = [
        pltpu.make_async_copy(source, target, in_sem.at[n])
        for n, (source, target) in enumerate(((gain_in, gain_ref), (tan_in, tan_ref), (order_in, order_ref), (flag_in, flag_ref)))
    ]
    for copy in inputs:
        copy.start()

    def peer(step):
        return {"grp": lax.rem(grp + (step + groups), groups)}

    partners = [place.neighbour(way * step) for step in range(1, max(*REACH, FAR) + 1) for way in (1, -1)]
    partners = partners + [sibling] + [peer(step) for step in range(1, groups)]
    barrier = pltpu.get_barrier_semaphore()
    for device in partners:
        pl.semaphore_signal(barrier, inc=1, device_id=device, device_id_type=MESH)


    def block(channel, chip, core):
        start = pl.multiple_of(lax.rem(chip, NEAR) * owned, owned)
        return all_ref.at[channel, chip // NEAR, core, pl.ds(start, owned), :]

    def block_copy(channel, origin, core, target, send_sem, recv_sem):
        chip = place.at(origin)
        return pltpu.make_async_remote_copy(
            src_ref=block(channel, chip, core), dst_ref=block(channel, chip, core),
            send_sem=send_sem, recv_sem=recv_sem, device_id=target, device_id_type=MESH,
        )

    def limit(way):
        return HALF if way > 0 else HALF - 1

    def pass_on(channel, way, done):
        copies = []
        for step in range(REACH[channel], 0, -1):
            if done + step <= limit(way):
                slot = HALF + way * (done + step)
                copies.append(block_copy(
                    channel, -way * done, place.core, place.neighbour(way * step), send_z.at[channel, slot], recv_z.at[channel, slot]
                ))
        return copies

    def core_copy(channel, core):
        return pltpu.make_async_remote_copy(
            src_ref=all_ref.at[channel, :, core], dst_ref=all_ref.at[channel, :, core],
            send_sem=send_s.at[channel], recv_sem=recv_s.at[channel], device_id=sibling, device_id_type=MESH,
        )

    def from_ring(channel, offset):
        slot = HALF + offset
        return block_copy(channel, -offset, place.core, sibling, send_z.at[channel, slot], recv_z.at[channel, slot])

    stages = [-(-HALF // reach) for reach in REACH]

    def begin_gather(channel):
        for pair in zip(pass_on(channel, 1, 0), pass_on(channel, -1, 0)):
            for copy in pair:
                copy.start()

    def gather_stage(channel, stage):
        for distance in range(min((stage + 1) * REACH[channel], HALF), stage * REACH[channel], -1):
            for way in (1, -1):
                if distance <= limit(way):
                    from_ring(channel, way * distance).wait_recv()
                    if distance % REACH[channel] == 0:
                        for copy in pass_on(channel, way, distance):
                            copy.start()
        if stage == stages[channel] - 1:
            core_copy(channel, place.core).start()

    def end_gather(channel):
        core_copy(channel, 1 - place.core).wait_recv()

    def to_peer(step):
        return pltpu.make_async_remote_copy(
            src_ref=peer_buf.at[0], dst_ref=peer_buf.at[step],
            send_sem=send_g.at[step], recv_sem=recv_g.at[step], device_id=peer(step), device_id_type=MESH,
        )

    def gather_sends(channel):
        copies = [core_copy(channel, place.core)]
        for way in (1, -1):
            for done in range(0, limit(way), REACH[channel]):
                copies += pass_on(channel, way, done)
        return copies


    def rows_of(step):
        chip = place.at(step)
        return chip // NEAR, pl.ds(pl.multiple_of(lax.rem(chip, NEAR) * owned, owned), owned)

    def swap(channel):
        return pltpu.make_async_remote_copy(
            src_ref=part_ref.at[channel, :, 1 - place.core], dst_ref=from_sib.at[channel],
            send_sem=send_w.at[channel], recv_sem=recv_w.at[channel], device_id=sibling, device_id_type=MESH,
        )

    def hop(source, target, channel, index, step):
        return pltpu.make_async_remote_copy(
            src_ref=source, dst_ref=target, send_sem=send_f.at[channel, index], recv_sem=recv_f.at[channel, index],
            device_id=place.neighbour(step), device_id_type=MESH,
        )

    def first_hops(channel):
        copies = [hop(up_ref.at[channel, 1, FAR - 1], far_up.at[channel], channel, FAR - 1, FAR)]
        for n in reversed(range(FAR - 1)):
            copies.append(hop(up_ref.at[channel, :, n], near_up.at[channel, n], channel, n, n + 1))
            copies.append(hop(down_ref.at[channel, :, n], near_down.at[channel, n], channel, FAR + n, -1 - n))
        return copies

    def second_hops(channel):
        return [
            hop(added_ref.at[channel, n], last_ref.at[channel, n], channel, 2 * FAR - 1 + n, (1 - 2 * n) * FAR) for n in range(2)
        ]

    def send_sums(channel):
        swap(channel).wait_recv()
        for step in range(1 - HALF, HALF + 1):
            run, rows = rows_of(step)
            value = part_ref[channel, run, place.core, rows, :] + from_sib[channel, run, rows, :]
            if step == 0:
                own_ref[channel] = value
            else:
                side, distance = (up_ref, step - 1) if step > 0 else (down_ref, -step - 1)
                side[channel, distance // FAR, distance % FAR] = value
        for copy in first_hops(channel):
            copy.start()

    def send_added(channel):
        for copy in first_hops(channel):
            copy.wait_recv()
        up = up_ref[channel, 0, FAR - 1] + far_up[channel]
        down = down_ref[channel, 0, FAR - 1]
        for n in range(FAR - 1):
            up = up + near_up[channel, n, 1]
            down = down + near_down[channel, n, 1]
        added_ref[channel, 0] = up
        added_ref[channel, 1] = down
        for copy in second_hops(channel):
            copy.start()

    def finish(channel):
        summed = own_ref[channel] + resid_ref[channel]
        for n in range(FAR - 1):
            summed = summed + near_up[channel, n, 0] + near_down[channel, n, 0]
        for n, copy in enumerate(second_hops(channel)):
            copy.wait_recv()
            summed = summed + last_ref[channel, n]
        out_ref[channel] = summed.T

    def sum_sends(channel):
        return [swap(channel)] + first_hops(channel) + second_hops(channel)


    basis = smooth_basis(channels * groups)

    def heights(group, channel):
        frequency = (group * channels + channel).astype(jnp.float32) * (2.0 / (channels * groups)) + (1.0 / (channels * groups) - 1.0)
        powers = [1.0]
        for _ in range(1, POLY):
            powers.append(powers[-1] * frequency)
        return [sum(line[k] * powers[k] for k in range(POLY) if abs(line[k]) > 1e-9) for line in basis]

    def consensus():
        moments = [jnp.zeros((owned, values), jnp.float32) for _ in range(POLY)]
        for step in range(groups):
            if step > 0:
                to_peer(step).wait_recv()
            origin = lax.rem(grp + (groups - step), groups)
            for source in range(channels):
                seen = peer_buf[step, source]
                for k, height in enumerate(heights(origin, source)):
                    moments[k] = moments[k] + height * seen
        for channel in range(channels):
            smooth = sum(height * moment for height, moment in zip(heights(grp, channel), moments))
            resid_ref[channel] = CONSENSUS_WEIGHT * (peer_buf[0, channel] - smooth)


    lane = lax.broadcasted_iota(jnp.int32, (ROWS, 128), 1)
    same_row = (lane & (ROWS - 1)) == lax.broadcasted_iota(jnp.int32, (ROWS, 128), 0)

    def as_mask(hit):
        return hit.astype(jnp.float32).astype(jnp.bfloat16)

    def one_hots():
        col_ids = order_ref[pl.ds(col, 1), :]
        row_ids = order_ref[pl.ds(row // 2, 1), :]
        row_ids = jnp.where(lax.rem(row, 2) == 1, pltpu.roll(row_ids, tile_rows, 1), row_ids)
        for n, ids in enumerate((col_ids, row_ids)):
            ids = jnp.broadcast_to(ids, (128, 128))
            turned = ids.astype(jnp.float32).T.astype(jnp.int32)
            count = (tile_cols, tile_rows)[n]
            for tile in range(stations // 128):
                spot = lax.broadcasted_iota(jnp.int32, (128, 128), 0) + tile * 128
                place_ref[tile, :, :, n * 128:(n + 1) * 128] = as_mask(ids == spot).reshape(2, near, 128)
            for core in range(2):
                for tile in range(stations // 256):
                    lane_in_core = lax.broadcasted_iota(jnp.int32, (128, 128), 1) + tile * 128
                    spot = (lane_in_core // near) * (2 * near) + core * near + lane_in_core % near
                    pick_ref[core, n * tile_cols:n * tile_cols + count, tile * 128:(tile + 1) * 128] = as_mask(turned == spot)[:count]

    def chosen_from(channel, core):
        held = all_ref[channel, :, core].reshape(stations // 2, 2 * values)
        return [dot(pick_ref[core], part) for part in split(held)]

    def choose_own(channel):
        for n, value in enumerate(chosen_from(channel, place.core)):
            chosen_ref[n] = value

    def prologue(channel):
        chosen = [chosen_ref[n] + value for n, value in enumerate(chosen_from(channel, 1 - place.core))]

        chosen_cols = chosen[0][:tile_cols] + chosen[1][:tile_cols]
        for array in range(2):
            turned = chosen_cols[:, array * values:(array + 1) * values].T.reshape(comps, directions, tile_cols)
            for line, entries in enumerate(conjugate_turned([turned[comp] for comp in range(comps)])):
                for end, entry in enumerate(entries):
                    for n, factor in enumerate(entry):
                        gj_ref[12 * array + 6 * line + 3 * end + n] = factor

        sides = [[
            one[tile_cols:, array * values:(array + 1) * values].T.reshape(comps, directions, tile_rows) for array in range(2)
        ] for one in chosen]
        for index in range(strips):
            lanes = slice(index * ROWS, (index + 1) * ROWS)
            for array in range(2):
                for line in range(2):
                    for part in range(2):
                        pieces = []
                        for side in sides:
                            for middle in range(2):
                                for other in range(2):
                                    value = side[array][4 * (part ^ other) + 2 * line + middle][:, lanes]
                                    pieces.append(-value if (part, other) == (0, 1) else value)
                        mix_ref[index, 4 * array + 2 * line + part] = jnp.concatenate(pieces, axis=1)
        col_ref[...] = jnp.zeros_like(col_ref)

    def strip(channel, index):
        rows = pl.ds(pl.multiple_of(index * ROWS, ROWS), ROWS)

        def forward(direction, change):
            here = slice(direction, direction + 1)
            coherent = [coh_ref[channel, comp, direction, rows, :] for comp in range(comps)]
            stacked = jnp.concatenate([
                jnp.concatenate([coherent[4 * part + 2 * middle], coherent[4 * part + 2 * middle + 1]], axis=1)
                for middle in range(2) for part in range(2)
            ], axis=0)
            mixing = jnp.concatenate([
                jnp.where(same_row, mix_ref[index, n, here, :], 0.0).astype(jnp.bfloat16) for n in range(8)
            ], axis=0)
            models = dot(mixing, jnp.concatenate([stacked, stacked], axis=0))

            def model(array):
                return [
                    models[ROWS * (4 * array + 2 * line + part):ROWS * (4 * array + 2 * line + part + 1), end * 128:(end + 1) * 128]
                    for part in range(2) for line in range(2) for end in range(2)
                ]

            model_left, tan_left = model(0), model(1)
            gain_j, tan_j = ([
                [[gj_ref[12 * array + 6 * line + 3 * end + n, here, :] for n in range(3)] for end in range(2)] for line in range(2)
            ] for array in range(2))
            for comp in range(comps):
                left_ref[comp, direction] = model_left[comp]
            model_right = products([(summed_parts([value.astype(jnp.float32) for value in coherent]), gain_j, False)])
            change = products([(summed_parts(tan_left), gain_j, False), (summed_parts(model_left), tan_j, False)], change)
            for part in range(2):
                for line in range(2):
                    for end in range(2):
                        for n, piece in enumerate(split(model_right[4 * part + 2 * line + end])):
                            lanes = slice((2 * n + end) * tile_cols, (2 * n + end + 1) * tile_cols)
                            right_ref[2 * line + part, direction, :, lanes] = piece
            return tuple(change)

        zero = jnp.zeros((ROWS, tile_cols), jnp.float32)
        change = (zero,) * comps
        for direction in range(directions):
            change = forward(direction, change)
        weight = flag_ref[rows, :].astype(jnp.float32)
        weighted = [value * weight for value in change]

        pieces = [split(value) for value in weighted]
        lines = [
            jnp.concatenate([
                jnp.concatenate([pieces[4 * part + 2 * line][n], pieces[4 * part + 2 * line + 1][n]], axis=1)
                for line in range(2) for part in range(2)
            ], axis=0) for n in range(2)
        ]
        lines = jnp.concatenate([
            jnp.concatenate([lines[0], lines[0]], axis=1), jnp.concatenate([lines[1], jnp.zeros_like(lines[1])], axis=1)
        ], axis=0)
        pairs = lax.dot_general(
            right_ref[...].reshape(4 * directions * ROWS, 4 * tile_cols), lines, (((1,), (1,)), ((), ())), preferred_element_type=jnp.float32
        ).reshape(4, directions, ROWS, 128)
        for n in range(4):
            row_ref[index, n] = jnp.sum(jnp.where(same_row[None], pairs[n], 0.0), axis=1)

        turned = conjugate_turned(weighted)
        for direction in range(directions):
            model_left = [left_ref[comp, direction] for comp in range(comps)]
            terms = products([(turned, summed_parts(model_left), True)])
            for comp in range(comps):
                folded = terms[comp][:8]
                for part in range(1, ROWS // 8):
                    folded = folded + terms[comp][8 * part:8 * part + 8]
                col_ref[comp, direction] += folded

    def epilogue(channel):
        sums = [[row_ref[index, n] for n in range(4)] for index in range(strips)]
        sums = [[value[:, :64] + value[:, 64:] for value in line] for line in sums]

        def cut(value, line, part):
            return value[:, (2 * line + part) * ROWS:(2 * line + part + 1) * ROWS]

        by_comp = []
        for part in range(2):
            for line in range(2):
                for end in range(2):
                    pieces = []
                    for value in sums:
                        if part == 0:
                            pieces.append(cut(value[2 * end], line, 0) + cut(value[2 * end + 1], line, 1))
                        else:
                            pieces.append(cut(value[2 * end], line, 1) - cut(value[2 * end + 1], line, 0))
                    by_comp.append(jnp.concatenate(pieces, axis=1))
        row_sums = jnp.concatenate(by_comp, axis=0)
        col_sums = jnp.sum(col_ref[...], axis=2).reshape(values, tile_cols)
        parts = split(jnp.concatenate([col_sums, row_sums], axis=1))

        def put(core):
            spots = place_ref[:, core].reshape(stations // 2, 256)[:, :tile_cols + tile_rows]
            placed = sum(lax.dot_general(spots, part, (((1,), (1,)), ((), ())), preferred_element_type=jnp.float32) for part in parts)
            part_ref[channel, :, core] = placed.reshape(stations // (2 * near), near, values)

        put(1 - place.core)
        swap(channel).start()
        put(place.core)


    inputs[0].wait()
    inputs[1].wait()
    own_start = pl.multiple_of(lax.rem(place.chip, NEAR) * owned, owned)
    for channel in range(channels):
        tan_t = tan_ref[channel].T
        peer_buf[0, channel] = tan_t
        own = all_ref.at[channel, place.chip // NEAR, place.core, pl.ds(own_start, owned), :]
        own[:, :values] = gain_ref[channel].T
        own[:, values:] = tan_t
    pl.semaphore_wait(barrier, len(partners))
    begin_gather(0)
    coherency = [pltpu.make_async_copy(coh_in.at[channel], coh_ref.at[channel], coh_sem.at[channel]) for channel in range(channels)]
    for copy in coherency:
        copy.start()
    inputs[2].wait()
    inputs[3].wait()
    one_hots()
    for stage in range(stages[0]):
        if stage == stages[0] - 1:
            begin_gather(1)
        gather_stage(0, stage)
    for step in range(1, groups):
        to_peer(step).start()
    for copy in coherency:
        copy.wait()

    def work(channel, _):
        choose_own(channel)
        for ready in range(channels):
            @pl.when(channel == ready)
            def _():
                end_gather(ready)

        prologue(channel)

        def one(index, _):
            for stage in range(stages[1]):
                @pl.when(jnp.logical_and(channel == 0, index == (strips - 1) * stage // (stages[1] - 1)))
                def _():
                    gather_stage(1, stage)

            @pl.when(jnp.logical_and(channel == 1, index == 1))
            def _():
                send_sums(0)

            strip(channel, index)
            return 0

        lax.fori_loop(0, strips, one, 0)
        epilogue(channel)
        return 0

    lax.fori_loop(0, channels, work, 0)
    send_sums(1)
    send_added(0)
    consensus()
    for copy in gather_sends(0) + gather_sends(1) + [to_peer(step) for step in range(1, groups)]:
        copy.wait_send()
    send_added(1)
    finish(0)
    for copy in sum_sends(0):
        copy.wait_send()
    finish(1)
    for copy in sum_sends(1):
        copy.wait_send()


def on_device(groups, coherency, station_gains, tangent, flag_mask, station_order):
    channels, comps, directions, tile_rows, tile_cols = coherency.shape
    owned = tangent.shape[3]
    stations = station_order.shape[0]
    values = comps * directions
    runs = CHIPS // NEAR
    near = NEAR * owned
    strips = tile_rows // ROWS
    vmem = pltpu.VMEM
    f32, bf16 = jnp.float32, jnp.bfloat16

    def sems(*shape):
        return pltpu.SemaphoreType.DMA(shape)

    hbm = pl.BlockSpec(memory_space=pltpu.HBM)
    result = pl.pallas_call(
        functools.partial(kernel, groups),
        out_shape=jax.ShapeDtypeStruct((channels, values, owned), f32),
        in_specs=[hbm] * 5,
        out_specs=pl.BlockSpec(memory_space=pltpu.VMEM),
        scratch_shapes=[
            vmem((channels, values, owned), f32),
            vmem((channels, values, owned), f32),
            vmem((stations // 128, 128), jnp.int32),
            vmem((tile_rows, tile_cols), jnp.int32),
            vmem(coherency.shape, bf16),
            vmem((channels, runs, 2, near, 2 * values), f32),
            vmem((groups, channels, owned, values), f32),
            vmem((channels, owned, values), f32),
            vmem((2, tile_cols + tile_rows, stations // 2), bf16),
            vmem((runs, 2, near, 256), bf16),
            vmem((2, tile_cols + tile_rows, 2 * values), f32),
            vmem((strips, comps, directions, 128), f32),
            vmem((24, directions, tile_cols), f32),
            vmem((comps, directions, ROWS, tile_cols), f32),
            vmem((4, directions, ROWS, 4 * tile_cols), bf16),
            vmem((strips, 4, directions, 128), f32),
            vmem((comps, directions, 8, tile_cols), f32),
            vmem((channels, runs, 2, near, values), f32),
            vmem((channels, runs, near, values), f32),
            vmem((channels, 2, FAR, owned, values), f32),
            vmem((channels, 2, FAR, owned, values), f32),
            vmem((channels, owned, values), f32),
            vmem((channels, FAR - 1, 2, owned, values), f32),
            vmem((channels, FAR - 1, 2, owned, values), f32),
            vmem((channels, owned, values), f32),
            vmem((channels, 2, owned, values), f32),
            vmem((channels, 2, owned, values), f32),
            sems(4), sems(channels),
            sems(channels, CHIPS + 1), sems(channels, CHIPS + 1), sems(channels), sems(channels),
            sems(groups), sems(groups), sems(channels), sems(channels),
            sems(channels, 2 * FAR + 1), sems(channels, 2 * FAR + 1),
        ],
        compiler_params=pltpu.CompilerParams(collective_id=0, has_side_effects=True, vmem_limit_bytes=24 << 20),
        name="hessian",
    )(
        *(pltpu.with_memory_space_constraint(value, pltpu.HBM) for value in (
            station_gains.reshape(channels, values, owned),
            tangent.reshape(channels, values, owned),
            station_order.reshape(stations // 128, 128),
            flag_mask,
            coherency,
        ))
    )
    return result.reshape(channels, comps, directions, owned)


def solution(mesh):
    in_specs = (
        P("grp", None, None, "row", "col"),
        P("grp", None, None, ("row", "col")),
        P("grp", None, None, ("row", "col")),
        P("row", "col"),
        P(),
    )
    out_specs = P("grp", None, None, ("row", "col"))
    return jax.shard_map(
        functools.partial(on_device, mesh.shape["grp"]),
        mesh=mesh, in_specs=in_specs, out_specs=out_specs, check_vma=False,
    )
```
